512 devices in a mesh: leaf: 32 (over y, x), near: 16 (over z, core).
Axes of the slice: x: 4, y: 8, z: 8, core: 2. Of those that a mesh axis runs over, the one named last changes fastest.
Arguments:
- input_point_values: bfloat16 [2048, 32, 256], P(('leaf', 'near')), may hold values from -6 to 6
- leaf_cluster_basis: bfloat16 [2048, 64, 256], P(('leaf', 'near')), may hold values from -0.375 to 0.375
- near_blocks: bfloat16 [2048, 7, 256, 256], P(('leaf', 'near')), may hold values from -0.125 to 0.125
- near_cols: int32 [2048, 7], P(('leaf', 'near')), may hold values from 0 to 2047, as said below
- leaf_transfer: bfloat16 [2048, 64, 64], P(('leaf', 'near')), may hold values from -0.375 to 0.375
- leaf_coupling: bfloat16 [8, 64, 64], replicated, may hold values from -0.3125 to 0.3125
- node_coupling: bfloat16 [512, 4, 64, 64], P(('leaf', 'near')), may hold values from -0.4375 to 0.4375
- level_transfer: bfloat16 [3, 2, 64, 64], replicated, may hold values from -0.5 to 0.5
- level_coupling: bfloat16 [3, 4, 64, 64], replicated, may hold values from -0.4375 to 0.4375
Outputs:
- product: float32 [2048, 32, 256], P(('leaf', 'near'))
The draws below stay inside these ranges and needn't reach their ends.
Inputs may be any that keep to these rules, and one draw needn't show every extreme that they name: `near_cols`: row i lists each leaf j with (j - i) mod 2048 or (i - j) mod 2048 at most 3 exactly once; the first is i itself.
All inputs are finite; a program needn't handle non-finite values.
Results may differ from the reference program's by a relative error of at most 0.0003.
Values may be sent and summed in bfloat16 or wider, within the bound.
No kernel may reach another device: no remote copies, remote signals or barrier semaphores. Data moves between devices by JAX's collectives and lax.ppermute only.
A program may use at most 64 MiB of HBM per device.

```python
import jax
import jax.numpy as jnp
from jax import lax

P_SIZE = 256
R = 64
RHS = 32
NREACH = 3
COARSE = 3
LEAF_DEV = 4
NEAR = 7
FAR_SIDE = 4
NODES = 512
LEAVES = 2048


def draw_near_cols(key, part):
    key = jax.random.fold_in(key, 11)
    candidates = jnp.concatenate([jnp.arange(-NREACH, 0), jnp.arange(1, NREACH + 1)]).astype(jnp.int32)
    scores = jax.random.randint(key, (LEAVES, 2 * NREACH), 0, 1 << 20) * (2 * NREACH) + jnp.arange(2 * NREACH, dtype=jnp.int32)[None, :]
    ranking = jnp.argsort(scores, axis=1)
    offsets = jnp.concatenate([jnp.zeros((LEAVES, 1), jnp.int32), candidates[ranking]], axis=1)
    rows_all = jnp.arange(LEAVES, dtype=jnp.int32)[:, None]
    return jnp.mod(rows_all + offsets, LEAVES).astype(jnp.int32)


def block_levels(rng, extent, cuts, low, largest):
    loudness = 1.0
    for axis_at, shards_of in cuts:
        heights = jax.random.uniform(jax.random.fold_in(jax.random.fold_in(rng, 6), axis_at), (shards_of,), jnp.float32, low / len(cuts), largest / len(cuts))
        loudness = loudness * jnp.repeat(jnp.exp(heights), extent[axis_at] // shards_of).reshape((-1,) + (1,) * (len(extent) - 1 - axis_at))
    return loudness


def bell_draw(stream_key, dims, width, limit, cuts=(), held_as=jnp.bfloat16):
    drawn = jax.random.normal(stream_key, dims, jnp.float32) * width
    if len(cuts) > 0:
        drawn = block_levels(stream_key, dims, cuts, -0.22, 0.18) * drawn
    return jnp.clip(drawn, min=-limit, max=limit).astype(held_as)


def setup_inputs(seed: int = 0) -> dict:
    keys = jax.random.split(jax.random.key(seed), 10)
    return {
        "input_point_values": bell_draw(keys[0], (LEAVES, RHS, P_SIZE), 1.0, 6.0, ((0, 512),)),
        "leaf_cluster_basis": bell_draw(keys[1], (LEAVES, R, P_SIZE), P_SIZE ** -0.5, 0.375, ((0, 512),)),
        "near_blocks": bell_draw(keys[2], (LEAVES, NEAR, P_SIZE, P_SIZE), (NEAR * P_SIZE) ** -0.5, 0.125, ((0, 512),)),
        "near_cols": draw_near_cols(jax.random.fold_in(keys[9], 71), 0),
        "leaf_transfer": bell_draw(keys[4], (LEAVES, R, R), (LEAF_DEV * R) ** -0.5, 0.375, ((0, 512),)),
        "leaf_coupling": bell_draw(keys[5], (2 * FAR_SIDE, R, R), ((3 * LEAF_DEV - NEAR) * R) ** -0.5, 0.3125),
        "node_coupling": bell_draw(keys[6], (NODES, 4, R, R), (3 * R) ** -0.5, 0.4375, ((0, 512),)),
        "level_transfer": bell_draw(keys[7], (COARSE, 2, R, R), (2 * R) ** -0.5, 0.5),
        "level_coupling": bell_draw(keys[8], (COARSE, 4, R, R), (3 * R) ** -0.5, 0.4375),
    }


OFFSETS = (-3, -2, 2, 3)
topmost_level = lax.Precision.HIGHEST


def parity_weight(count_nodes, position_index):
    parity = jnp.arange(count_nodes, dtype=jnp.int32) % 2
    if position_index == 0:
        return (parity == 1).astype(jnp.float32)
    if position_index == 3:
        return (parity == 0).astype(jnp.float32)
    return jnp.ones((count_nodes,), jnp.float32)


def near_part(input_point_values, near_blocks, near_cols):
    span = LEAF_DEV * 8

    def one_block(block_index):
        start = (block_index * span).astype(jnp.int32)
        blocks = lax.dynamic_slice_in_dim(near_blocks, start, span, 0).astype(jnp.float32)
        columns = lax.dynamic_slice_in_dim(near_cols, start, span, 0)
        picked = jnp.take(input_point_values, columns, axis=0).astype(jnp.float32)
        return jnp.einsum('lkpq,lksq->lsp', blocks, picked, precision=topmost_level)

    pieces = lax.map(one_block, jnp.arange(LEAVES // span, dtype=jnp.int32))
    return pieces.reshape(LEAVES, RHS, P_SIZE)


def reference(input_point_values, leaf_cluster_basis, near_blocks, near_cols, leaf_transfer, leaf_coupling, node_coupling, level_transfer, level_coupling):
    widened_basis = leaf_cluster_basis.astype(jnp.float32)
    leaf_multipoles = jnp.einsum('zcw,znw->zcn', input_point_values.astype(jnp.float32), widened_basis, precision=topmost_level)
    leaf_expansion = leaf_transfer.astype(jnp.float32)
    raised_moments = jnp.einsum('znj,zjp->znp', leaf_multipoles, leaf_expansion, precision=topmost_level)
    moments_zero = raised_moments.reshape(NODES, LEAF_DEV, RHS, R).sum(axis=1)
    transfer = level_transfer.astype(jnp.float32)
    coupling = level_coupling.astype(jnp.float32)
    levels = [moments_zero]
    for height in range(COARSE):
        previous = levels[-1]
        upper = jnp.einsum('nsr,rq->nsq', previous[0::2], transfer[height, 0], precision=topmost_level)
        upper = upper + jnp.einsum('nsr,rq->nsq', previous[1::2], transfer[height, 1], precision=topmost_level)
        levels.append(upper)
    locals_all = []
    for height in range(COARSE + 1):
        moments = levels[height]
        count_nodes = moments.shape[0]
        accum = jnp.zeros_like(moments)
        for position_index, offset in enumerate(OFFSETS):
            interaction_partner = jnp.roll(moments, -offset, axis=0)
            if height == 0:
                matrices = node_coupling[:, position_index].astype(jnp.float32)
                summand = jnp.einsum('nsr,nrq->nsq', interaction_partner, matrices, precision=topmost_level)
            else:
                summand = jnp.einsum('nsr,rq->nsq', interaction_partner, coupling[height - 1, position_index], precision=topmost_level)
            summand = summand * parity_weight(count_nodes, position_index)[:, None, None]
            accum = accum + summand
        locals_all.append(accum)
    fields = locals_all[COARSE]
    for height in reversed(range(COARSE)):
        count_nodes = locals_all[height].shape[0]
        selected = transfer[height][jnp.arange(count_nodes) % 2]
        parents = jnp.repeat(fields, 2, axis=0)
        fields = locals_all[height] + jnp.einsum('nsq,nrq->nsr', parents, selected, precision=topmost_level)
    leaf_potential = jnp.einsum('nsq,nlrq->nlsr', fields, leaf_expansion.reshape(NODES, LEAF_DEV, R, R), precision=topmost_level)
    leaf_potential = leaf_potential.reshape(LEAVES, RHS, R)
    widened_coupling = leaf_coupling.astype(jnp.float32)
    leaf_index = jnp.arange(LEAVES, dtype=jnp.int32)
    for position_index in range(2 * FAR_SIDE):
        if position_index < FAR_SIDE:
            offset = -(NREACH + 1 + position_index)
        else:
            offset = NREACH + 1 + position_index - FAR_SIDE
        target = leaf_index + offset
        gap = jnp.floor_divide(target, LEAF_DEV) - jnp.floor_divide(leaf_index, LEAF_DEV)
        valid = (jnp.abs(gap) <= 1).astype(jnp.float32)
        interaction_partner = jnp.roll(leaf_multipoles, -offset, axis=0)
        summand = jnp.einsum('ejp,pb->ejb', interaction_partner, widened_coupling[position_index], precision=topmost_level)
        leaf_potential = leaf_potential + summand * valid[:, None, None]
    distant_sum = jnp.einsum('hve,hea->hva', leaf_potential, widened_basis, precision=topmost_level)
    return distant_sum + near_part(input_point_values, near_blocks, near_cols)
```

```python
import jax
import jax.numpy as jnp
from jax import lax
from jax.experimental import pallas as pl
from jax.experimental.pallas import tpu as pltpu
from jax.sharding import PartitionSpec as P

AXES = ("leaf", "near")
NREACH = 3
OFFSETS = (-3, -2, 2, 3)
CHIPS = 8
BF16, F32 = jnp.bfloat16, jnp.float32
VMEM = pl.BlockSpec(memory_space=pltpu.VMEM)
HBM = pl.BlockSpec(memory_space=pltpu.HBM)


def dot(a, b):
    return lax.dot_general(a, b, (((1,), (0,)), ((), ())), preferred_element_type=F32)


def dot_nt(a, b):
    return lax.dot_general(a, b, (((1,), (1,)), ((), ())), preferred_element_type=F32)


def halves(value):
    high = value.astype(BF16)
    low = (value - high.astype(F32)).astype(BF16)
    return jnp.concatenate([high, low], axis=1)


def stacked(weights, axis):
    return jnp.concatenate([w for w in weights for _ in range(2)], axis=axis)


def load(sources, targets, semaphores):
    copies = [
        pltpu.make_async_copy(source, target, semaphores.at[i])
        for i, (source, target) in enumerate(zip(sources, targets, strict=True))
    ]
    for copy in copies:
        copy.start()
    return copies


def moments_kernel(
    x_hbm, basis_hbm, transfer_hbm, x_ref, basis_ref, transfer_ref, package_ref, semaphores
):
    odd = lax.axis_index("near") % 2
    copies = load(
        (x_hbm, basis_hbm, transfer_hbm), (x_ref, basis_ref, transfer_ref), semaphores
    )
    copies[0].wait()
    package_ref[0:3] = x_ref[pl.ds(1 - odd, 3)]
    copies[1].wait()
    parts = [halves(dot_nt(x_ref[j], basis_ref[j])) for j in range(4)]
    package_ref[3] = jnp.concatenate(parts[:2], axis=1)
    package_ref[4] = jnp.concatenate(parts[2:], axis=1)
    copies[2].wait()
    weights = stacked([transfer_ref[j] for j in range(4)], 0)
    node = halves(dot(jnp.concatenate(parts, axis=1), weights))
    package_ref[5] = jnp.concatenate([node, jnp.zeros_like(node)], axis=1)


def weights_kernel(
    level_hbm, coupling_hbm, leaf_hbm, node_hbm, up_ref, down_ref, coupling_ref, leaf_ref, node_ref,
    level, coupling, leaf, node, semaphores,
):
    near = lax.axis_index("near")
    copies = load(
        (level_hbm, coupling_hbm, leaf_hbm, node_hbm), (level, coupling, leaf, node), semaphores
    )
    copies[0].wait()
    for c in range(3):
        up_ref[c] = stacked([level[c, 0], level[c, 1]], 0)
        down_ref[c] = stacked([level[c, (near >> c) % 2]], 1)
    copies[1].wait()
    for c in range(3):
        coupling_ref[c] = stacked([coupling[c, k] for k in range(4)], 0)
    copies[2].wait()
    leaf_ref[...] = stacked([leaf[k] for k in range(8)], 0)
    copies[3].wait()
    node_ref[...] = stacked([node[0, k] for k in range(4)], 0)


def pair_kernel(x_ref, mine_ref, sibling_ref, up_ref, chunk_ref, next_ref, nodes_ref):
    odd = lax.axis_index("near") % 2
    mine = mine_ref[5][:, :128]
    sibling = sibling_ref[5][:, :128]
    even_node = jnp.where(odd == 1, sibling, mine)
    odd_node = jnp.where(odd == 1, mine, sibling)
    chip = halves(dot(jnp.concatenate([even_node, odd_node], axis=1), up_ref[0]))
    for j in range(chunk_ref.shape[0]):
        chunk_ref[j] = chip
    nodes_ref[...] = jnp.concatenate([mine, sibling], axis=1)
    next_ref[0:3] = x_ref[pl.ds(odd, 3)]
    next_ref[3:5] = mine_ref[3:5]
    next_ref[5] = jnp.concatenate([sibling, sibling], axis=1)


def levels_kernel(
    chips_ref, up_ref, down_ref, coupling_ref, send_ref, own_ref, quads, octets
):
    near = lax.axis_index("near")
    side = lax.axis_index("leaf") % 2
    z = near // 2
    rows = [jnp.concatenate([chips_ref[2 * q], chips_ref[2 * q + 1]], axis=1) for q in range(8)]
    second = halves(dot(jnp.concatenate(rows, axis=0), up_ref[1])).reshape(8, 32, 128)
    quads[...] = second
    rows = [jnp.concatenate([second[2 * q], second[2 * q + 1]], axis=1) for q in range(4)]
    third = halves(dot(jnp.concatenate(rows, axis=0), up_ref[2])).reshape(4, 32, 128)
    octets[...] = third
    own = side * CHIPS + z
    other = jnp.where(side == 0, z - CHIPS, z + 2 * CHIPS)
    fields = []
    for c, table in ((0, chips_ref), (1, quads), (2, octets)):
        count = table.shape[0]
        parity = (z >> c) % 2
        rows = []
        for target in (own, other):
            node = target >> c
            blocks = []
            for k, offset in enumerate(OFFSETS):
                partner = node + offset
                valid = (partner >= 0) & (partner < count)
                if k == 0:
                    valid = valid & (parity == 1)
                if k == 3:
                    valid = valid & (parity == 0)
                block = table[jnp.clip(partner, 0, count - 1)]
                blocks.append(jnp.where(valid, block, jnp.zeros_like(block)))
            rows.append(jnp.concatenate(blocks, axis=1))
        fields.append(dot(jnp.concatenate(rows, axis=0), coupling_ref[c]))
    field = fields[2]
    for c in (2, 1, 0):
        field = dot_nt(halves(field), down_ref[c])
        if c:
            field = field + fields[c - 1]
    own_ref[...] = field[:32]
    send_ref[...] = halves(field[32:])


def near_kernel(
    x_ref, sibling_ref, next_ref, nodes_ref, own_ref, leaf_ref, node_ref, cols_hbm, blocks_hbm,
    near_ref, far_ref, field_ref, window, cols, blocks, semaphores,
):
    copies = load(
        [blocks_hbm.at[j] for j in range(4)] + [cols_hbm],
        [blocks.at[j] for j in range(4)] + [cols],
        semaphores,
    )
    near = lax.axis_index("near")
    odd = near % 2
    first = (lax.axis_index("leaf") * (2 * CHIPS) + near) * 4 - NREACH
    is_odd = odd == 1
    window[3:7] = x_ref[...]
    window[0:3] = jnp.where(is_odd, sibling_ref[0:3], next_ref[0:3])
    window[7:10] = jnp.where(is_odd, next_ref[0:3], sibling_ref[0:3])
    zero = jnp.zeros((32, 128), BF16)
    left, right = [], []
    for pair in (3, 4):
        from_sibling, from_next = sibling_ref[pair], next_ref[pair]
        before = jnp.where(is_odd, from_sibling, from_next)
        after = jnp.where(is_odd, from_next, from_sibling)
        left += [before[:, :128], before[:, 128:]]
        right += [after[:, :128], after[:, 128:]]
    rows = []
    for j in range(4):
        row = [left[j - k] if k <= j else zero for k in range(4)]
        row += [right[j + k] if k <= 3 - j else zero for k in range(4)]
        rows.append(jnp.concatenate(row, axis=1))
    coupled = dot(jnp.concatenate(rows, axis=0), leaf_ref[...])
    for j in range(4):
        far_ref[j] = coupled[32 * j : 32 * j + 32]
    direct = nodes_ref[:, :128]
    beside = nodes_ref[:, 128:]
    adjacent = next_ref[5][:, :128]
    row = [
        jnp.where(is_odd, direct, zero),
        jnp.where(is_odd, beside, adjacent),
        jnp.where(is_odd, adjacent, beside),
        jnp.where(is_odd, zero, direct),
    ]
    field_ref[...] = own_ref[...] + dot(jnp.concatenate(row, axis=1), node_ref[...])
    copies[4].wait()
    for j in range(4):
        total = None
        copies[j].wait()
        for k in range(7):
            place = (cols[j, k] - first) & 2047
            term = dot_nt(window[place], blocks[j, k])
            total = term if total is None else total + term
        near_ref[j] = total


def product_kernel(near_ref, far_ref, field_ref, given_ref, transfer_ref, basis_ref, out_ref):
    given = given_ref[...].astype(F32)
    field = halves(field_ref[...] + given[:, :64] + given[:, 64:])
    for j in range(4):
        leaf_field = dot_nt(field, stacked([transfer_ref[j]], 1)) + far_ref[j]
        out_ref[j] = dot(halves(leaf_field), stacked([basis_ref[j]], 0)) + near_ref[j]


def call(kernel, out, specs, scratch=(), flops=0, size=0):
    return pl.pallas_call(
        kernel,
        out_shape=[jax.ShapeDtypeStruct(shape, dtype) for shape, dtype in out],
        in_specs=specs,
        out_specs=[VMEM] * len(out),
        scratch_shapes=list(scratch),
        compiler_params=pltpu.CompilerParams(vmem_limit_bytes=16 << 20),
        cost_estimate=pl.CostEstimate(flops=flops, bytes_accessed=size, transcendentals=0),
    )


def in_hbm(*arrays):
    return [pltpu.with_memory_space_constraint(array, pltpu.HBM) for array in arrays]


def permute(value, partner):
    members = lax.axis_size(AXES)
    return lax.ppermute(value, AXES, [(i, partner(i) % members) for i in range(members)])


def local(
    input_point_values,
    leaf_cluster_basis,
    near_blocks,
    near_cols,
    leaf_transfer,
    leaf_coupling,
    node_coupling,
    level_transfer,
    level_coupling,
):
    block = lax.axis_size("near")
    x, basis, transfer, package = call(
        moments_kernel,
        [((4, 32, 256), BF16), ((4, 64, 256), BF16), ((4, 64, 64), BF16), ((6, 32, 256), BF16)],
        [HBM] * 3,
        [pltpu.SemaphoreType.DMA((3,))],
    )(*in_hbm(input_point_values, leaf_cluster_basis, leaf_transfer))
    sibling = permute(package, lambda i: i ^ 1)
    up, down, coupling, leaf, node = call(
        weights_kernel,
        [
            ((3, 256, 64), BF16),
            ((3, 64, 128), BF16),
            ((3, 512, 64), BF16),
            ((1024, 64), BF16),
            ((512, 64), BF16),
        ],
        [HBM] * 4,
        [
            pltpu.VMEM((3, 2, 64, 64), BF16),
            pltpu.VMEM((3, 4, 64, 64), BF16),
            pltpu.VMEM((8, 64, 64), BF16),
            pltpu.VMEM((1, 4, 64, 64), BF16),
            pltpu.SemaphoreType.DMA((4,)),
        ],
        size=2_000_000,
    )(*in_hbm(level_transfer, level_coupling, leaf_coupling, node_coupling))
    chunk, package, nodes = call(
        pair_kernel,
        [((16, 32, 128), BF16), ((6, 32, 256), BF16), ((32, 256), BF16)],
        [VMEM] * 4,
    )(x, package, sibling, up)
    groups = [
        [2 * block * pair + block * side + 2 * z + core for side in range(2) for z in range(CHIPS)]
        for pair in range(lax.axis_size("leaf") // 2)
        for core in range(2)
    ]
    chips = lax.all_to_all(chunk, AXES, 0, 0, axis_index_groups=groups)
    after = permute(package, lambda i: i + 1 if i % 2 else i - 1)
    nodes = permute(nodes, lambda i: i - 3 if i % 2 else i + 3)
    send, own = call(
        levels_kernel,
        [((32, 128), BF16), ((32, 64), F32)],
        [VMEM] * 4,
        [pltpu.VMEM((8, 32, 128), BF16), pltpu.VMEM((4, 32, 128), BF16)],
    )(chips, up, down, coupling)
    given = permute(send, lambda i: i + block if i // block % 2 else i - block)
    near, far, field = call(
        near_kernel,
        [((4, 32, 256), F32), ((4, 32, 64), F32), ((32, 64), F32)],
        [VMEM] * 7 + [HBM] * 2,
        [
            pltpu.VMEM((10, 32, 256), BF16),
            pltpu.SMEM((4, 7), jnp.int32),
            pltpu.VMEM((4, 7, 256, 256), BF16),
            pltpu.SemaphoreType.DMA((5,)),
        ],
        flops=200_000_000,
        size=4_000_000,
    )(x, sibling, after, nodes, own, leaf, node, *in_hbm(near_cols, near_blocks))
    (out,) = call(product_kernel, [((4, 32, 256), F32)], [VMEM] * 6)(
        near, far, field, given, transfer, basis
    )
    return out


def solution(mesh):
    spread = P(AXES)
    placed = (spread, spread, spread, spread, spread, P(), spread, P(), P())
    return jax.shard_map(
        local, mesh=mesh, in_specs=placed, out_specs=spread, check_vma=False
    )
```

```python
import jax
import jax.numpy as jnp
from jax import lax
from jax.experimental import pallas as pl
from jax.experimental.pallas import tpu as pltpu
from jax.sharding import PartitionSpec as P

AXES = ("leaf", "near")
NREACH = 3
OFFSETS = (-3, -2, 2, 3)
CHIPS = 8
EARLY = 6
BF16, F32 = jnp.bfloat16, jnp.float32
VMEM = pl.BlockSpec(memory_space=pltpu.VMEM)
HBM = pl.BlockSpec(memory_space=pltpu.HBM)


def dot(a, b):
    return lax.dot_general(a, b, (((1,), (0,)), ((), ())), preferred_element_type=F32)


def dot_nt(a, b):
    return lax.dot_general(a, b, (((1,), (1,)), ((), ())), preferred_element_type=F32)


def halves(value):
    high = value.astype(BF16)
    low = (value - high.astype(F32)).astype(BF16)
    return jnp.concatenate([high, low], axis=1)


def stacked(weights, axis):
    return jnp.concatenate([w for w in weights for _ in range(2)], axis=axis)


def load(sources, targets, semaphores):
    copies = [
        pltpu.make_async_copy(source, target, semaphores.at[i])
        for i, (source, target) in enumerate(zip(sources, targets, strict=True))
    ]
    for copy in copies:
        copy.start()
    return copies


def moments_kernel(
    x_hbm, basis_hbm, transfer_hbm, x_ref, basis_ref, transfer_ref, package_ref, semaphores
):
    odd = lax.axis_index("near") % 2
    copies = load(
        (x_hbm, basis_hbm, transfer_hbm), (x_ref, basis_ref, transfer_ref), semaphores
    )
    copies[0].wait()
    package_ref[0:3] = x_ref[pl.ds(1 - odd, 3)]
    copies[1].wait()
    parts = [halves(dot_nt(x_ref[j], basis_ref[j])) for j in range(4)]
    package_ref[3] = jnp.concatenate(parts[:2], axis=1)
    package_ref[4] = jnp.concatenate(parts[2:], axis=1)
    copies[2].wait()
    weights = stacked([transfer_ref[j] for j in range(4)], 0)
    node = halves(dot(jnp.concatenate(parts, axis=1), weights))
    package_ref[5] = jnp.concatenate([node, jnp.zeros_like(node)], axis=1)


def weights_kernel(
    level_hbm, coupling_hbm, leaf_hbm, node_hbm, up_ref, down_ref, coupling_ref, leaf_ref, node_ref,
    level, coupling, leaf, node, semaphores,
):
    near = lax.axis_index("near")
    copies = load(
        (level_hbm, coupling_hbm, leaf_hbm, node_hbm), (level, coupling, leaf, node), semaphores
    )
    copies[0].wait()
    for c in range(3):
        up_ref[c] = stacked([level[c, 0], level[c, 1]], 0)
        down_ref[c] = stacked([level[c, (near >> c) % 2]], 1)
    copies[1].wait()
    for c in range(3):
        coupling_ref[c] = stacked([coupling[c, k] for k in range(4)], 0)
    copies[2].wait()
    leaf_ref[...] = stacked([leaf[k] for k in range(8)], 0)
    copies[3].wait()
    node_ref[...] = stacked([node[0, k] for k in range(4)], 0)


def pair_kernel(x_ref, mine_ref, sibling_ref, up_ref, chunk_ref, next_ref, pairs_ref):
    odd = lax.axis_index("near") % 2
    mine = mine_ref[5][:, :128]
    sibling = sibling_ref[5][:, :128]
    even_node = jnp.where(odd == 1, sibling, mine)
    odd_node = jnp.where(odd == 1, mine, sibling)
    chip = halves(dot(jnp.concatenate([even_node, odd_node], axis=1), up_ref[0]))
    for j in range(chunk_ref.shape[0]):
        chunk_ref[j] = chip
    next_ref[0:3] = x_ref[pl.ds(odd, 3)]
    next_ref[3:5] = mine_ref[3:5]
    next_ref[5] = jnp.concatenate([mine, sibling], axis=1)
    pairs_ref[...] = jnp.concatenate([mine, sibling], axis=1)


def levels_kernel(
    chips_ref, up_ref, down_ref, coupling_ref, send_ref, own_ref, quads, octets
):
    near = lax.axis_index("near")
    side = (lax.axis_index("leaf") + 1) % 2
    z = near // 2
    rows = [jnp.concatenate([chips_ref[2 * q], chips_ref[2 * q + 1]], axis=1) for q in range(8)]
    second = halves(dot(jnp.concatenate(rows, axis=0), up_ref[1])).reshape(8, 32, 128)
    quads[...] = second
    rows = [jnp.concatenate([second[2 * q], second[2 * q + 1]], axis=1) for q in range(4)]
    third = halves(dot(jnp.concatenate(rows, axis=0), up_ref[2])).reshape(4, 32, 128)
    octets[...] = third
    own = side * CHIPS + z
    other = jnp.where(side == 0, z - CHIPS, z + 2 * CHIPS)
    fields = []
    for c, table in ((0, chips_ref), (1, quads), (2, octets)):
        count = table.shape[0]
        parity = (z >> c) % 2
        rows = []
        for target in (own, other):
            node = target >> c
            blocks = []
            for k, offset in enumerate(OFFSETS):
                partner = node + offset
                valid = (partner >= 0) & (partner < count)
                if k == 0:
                    valid = valid & (parity == 1)
                if k == 3:
                    valid = valid & (parity == 0)
                block = table[jnp.clip(partner, 0, count - 1)]
                blocks.append(jnp.where(valid, block, jnp.zeros_like(block)))
            rows.append(jnp.concatenate(blocks, axis=1))
        fields.append(dot(jnp.concatenate(rows, axis=0), coupling_ref[c]))
    field = fields[2]
    for c in (2, 1, 0):
        field = dot_nt(halves(field), down_ref[c])
        if c:
            field = field + fields[c - 1]
    own_ref[...] = field[:32]
    send_ref[...] = halves(field[32:])


def near_all(window, cols, blocks, copies, near_ref, first):
    copies[4].wait()
    for j in range(4):
        total = None
        copies[j].wait()
        for k in range(7):
            place = (cols[j, k] - first) & 2047
            term = dot_nt(window[place], blocks[j, k])
            total = term if total is None else total + term
        near_ref[j] = total


def load_near(cols_hbm, blocks_hbm, cols, blocks, semaphores):
    return load(
        [blocks_hbm.at[j] for j in range(4)] + [cols_hbm],
        [blocks.at[j] for j in range(4)] + [cols],
        semaphores,
    )


def position():
    near = lax.axis_index("near")
    first = (lax.axis_index("leaf") * (2 * CHIPS) + near) * 4 - NREACH
    return near % 2 == 1, near < EARLY, first


def early_kernel(
    x_ref, sibling_ref, cols_hbm, blocks_hbm, near_ref, window, cols, blocks, semaphores
):
    is_odd, early, first = position()

    @pl.when(early)
    def _():
        copies = load_near(cols_hbm, blocks_hbm, cols, blocks, semaphores)
        window[3:7] = x_ref[...]
        halo = sibling_ref[0:3]
        none = jnp.zeros_like(halo)
        window[0:3] = jnp.where(is_odd, halo, none)
        window[7:10] = jnp.where(is_odd, none, halo)
        near_all(window, cols, blocks, copies, near_ref, first)


def near_kernel(
    x_ref, sibling_ref, next_ref, leaf_ref, begun_ref, cols_hbm, blocks_hbm,
    near_ref, far_ref, window, cols, blocks, semaphores,
):
    is_odd, early, first = position()

    @pl.when(early)
    def _():
        copy = pltpu.make_async_copy(cols_hbm, cols, semaphores.at[4])
        copy.start()
        near_ref[...] = begun_ref[...]
        copy.wait()
        rest = [(j, t) for j in range(3) for t in range(j, 3)]
        leaves = [jnp.where(is_odd, 3 - j, j) for j in range(3)]
        copies = []
        for slot, (j, t) in enumerate(rest):
            place = jnp.where(is_odd, 9 - t, t)
            k = sum(
                jnp.where(((cols[leaves[j], i] - first) & 2047) == place, i, 0) for i in range(7)
            )
            copies.append(
                pltpu.make_async_copy(
                    blocks_hbm.at[leaves[j], k], blocks.at[0, slot], semaphores.at[slot]
                )
            )
            copies[-1].start()
        for slot, (j, t) in enumerate(rest):
            copies[slot].wait()
            place = jnp.where(is_odd, 2 - t, t)
            near_ref[leaves[j]] += dot_nt(next_ref[place], blocks[0, slot])

    @pl.when(jnp.logical_not(early))
    def _():
        copies = load_near(cols_hbm, blocks_hbm, cols, blocks, semaphores)
        window[3:7] = x_ref[...]
        window[0:3] = jnp.where(is_odd, sibling_ref[0:3], next_ref[0:3])
        window[7:10] = jnp.where(is_odd, next_ref[0:3], sibling_ref[0:3])
        near_all(window, cols, blocks, copies, near_ref, first)

    zero = jnp.zeros((32, 128), BF16)
    left, right = [], []
    for pair in (3, 4):
        from_sibling, from_next = sibling_ref[pair], next_ref[pair]
        before = jnp.where(is_odd, from_sibling, from_next)
        after = jnp.where(is_odd, from_next, from_sibling)
        left += [before[:, :128], before[:, 128:]]
        right += [after[:, :128], after[:, 128:]]
    rows = []
    for j in range(4):
        row = [left[j - k] if k <= j else zero for k in range(4)]
        row += [right[j + k] if k <= 3 - j else zero for k in range(4)]
        rows.append(jnp.concatenate(row, axis=1))
    coupled = dot(jnp.concatenate(rows, axis=0), leaf_ref[...])
    for j in range(4):
        far_ref[j] = coupled[32 * j : 32 * j + 32]


def product_kernel(
    near_ref, far_ref, own_ref, given_ref, next_ref, facing_ref, node_ref, transfer_ref, basis_ref,
    out_ref,
):
    is_odd = lax.axis_index("near") % 2 == 1
    zero = jnp.zeros((32, 128), BF16)
    adjacent = next_ref[5][:, 128:]
    distant, close = facing_ref[:, :128], facing_ref[:, 128:]
    row = [
        jnp.where(is_odd, distant, zero),
        jnp.where(is_odd, close, adjacent),
        jnp.where(is_odd, adjacent, close),
        jnp.where(is_odd, zero, distant),
    ]
    given = given_ref[...].astype(F32)
    field = own_ref[...] + dot(jnp.concatenate(row, axis=1), node_ref[...])
    field = halves(field + given[:, :64] + given[:, 64:])
    for j in range(4):
        leaf_field = dot_nt(field, stacked([transfer_ref[j]], 1)) + far_ref[j]
        out_ref[j] = dot(halves(leaf_field), stacked([basis_ref[j]], 0)) + near_ref[j]


def call(kernel, out, specs, scratch=(), flops=0, size=0):
    return pl.pallas_call(
        kernel,
        out_shape=[jax.ShapeDtypeStruct(shape, dtype) for shape, dtype in out],
        in_specs=specs,
        out_specs=[VMEM] * len(out),
        scratch_shapes=list(scratch),
        compiler_params=pltpu.CompilerParams(vmem_limit_bytes=16 << 20),
        cost_estimate=pl.CostEstimate(flops=flops, bytes_accessed=size, transcendentals=0),
    )


def in_hbm(*arrays):
    return [pltpu.with_memory_space_constraint(array, pltpu.HBM) for array in arrays]


def permute(value, partner):
    members = lax.axis_size(AXES)
    return lax.ppermute(value, AXES, [(i, partner(i) % members) for i in range(members)])


def local(
    input_point_values,
    leaf_cluster_basis,
    near_blocks,
    near_cols,
    leaf_transfer,
    leaf_coupling,
    node_coupling,
    level_transfer,
    level_coupling,
):
    block = lax.axis_size("near")
    x, basis, transfer, package = call(
        moments_kernel,
        [((4, 32, 256), BF16), ((4, 64, 256), BF16), ((4, 64, 64), BF16), ((6, 32, 256), BF16)],
        [HBM] * 3,
        [pltpu.SemaphoreType.DMA((3,))],
    )(*in_hbm(input_point_values, leaf_cluster_basis, leaf_transfer))
    sibling = permute(package, lambda i: i ^ 1)
    up, down, coupling, leaf, node = call(
        weights_kernel,
        [
            ((3, 256, 64), BF16),
            ((3, 64, 128), BF16),
            ((3, 512, 64), BF16),
            ((1024, 64), BF16),
            ((512, 64), BF16),
        ],
        [HBM] * 4,
        [
            pltpu.VMEM((3, 2, 64, 64), BF16),
            pltpu.VMEM((3, 4, 64, 64), BF16),
            pltpu.VMEM((8, 64, 64), BF16),
            pltpu.VMEM((1, 4, 64, 64), BF16),
            pltpu.SemaphoreType.DMA((4,)),
        ],
        size=2_000_000,
    )(*in_hbm(level_transfer, level_coupling, leaf_coupling, node_coupling))
    chunk, package, pairs = call(
        pair_kernel,
        [((16, 32, 128), BF16), ((6, 32, 256), BF16), ((32, 256), BF16)],
        [VMEM] * 4,
    )(x, package, sibling, up)
    (begun,) = call(
        early_kernel,
        [((4, 32, 256), F32)],
        [VMEM] * 2 + [HBM] * 2,
        [
            pltpu.VMEM((10, 32, 256), BF16),
            pltpu.SMEM((4, 7), jnp.int32),
            pltpu.VMEM((4, 7, 256, 256), BF16),
            pltpu.SemaphoreType.DMA((5,)),
        ],
    )(x, sibling, *in_hbm(near_cols, near_blocks))
    chunk, begun = lax.optimization_barrier((chunk, begun))
    groups = [
        [(2 * block * pair + block * (side - 1) + 2 * z + core) % 512 for side in range(2) for z in range(CHIPS)]
        for pair in range(lax.axis_size("leaf") // 2)
        for core in range(2)
    ]
    chips = lax.all_to_all(chunk, AXES, 0, 0, axis_index_groups=groups)
    after = permute(package, lambda i: i + 1 if i % 2 else i - 1)
    facing = permute(pairs, lambda i: i - 3 if i % 2 else i + 3)
    send, own = call(
        levels_kernel,
        [((32, 128), BF16), ((32, 64), F32)],
        [VMEM] * 4,
        [pltpu.VMEM((8, 32, 128), BF16), pltpu.VMEM((4, 32, 128), BF16)],
    )(chips, up, down, coupling)
    given = permute(send, lambda i: i - block if i // block % 2 else i + block)

    near, far = call(
        near_kernel,
        [((4, 32, 256), F32), ((4, 32, 64), F32)],
        [VMEM] * 5 + [HBM] * 2,
        [
            pltpu.VMEM((10, 32, 256), BF16),
            pltpu.SMEM((4, 7), jnp.int32),
            pltpu.VMEM((4, 7, 256, 256), BF16),
            pltpu.SemaphoreType.DMA((6,)),
        ],
        flops=200_000_000,
        size=4_000_000,
    )(x, sibling, after, leaf, begun, *in_hbm(near_cols, near_blocks))
    (out,) = call(product_kernel, [((4, 32, 256), F32)], [VMEM] * 9)(
        near, far, own, given, after, facing, node, transfer, basis
    )
    return out


def solution(mesh):
    spread = P(AXES)
    placed = (spread, spread, spread, spread, spread, P(), spread, P(), P())
    return jax.shard_map(
        local, mesh=mesh, in_specs=placed, out_specs=spread, check_vma=False
    )
```

```python
import jax
import jax.numpy as jnp
from jax import lax
from jax.experimental import pallas as pl
from jax.experimental.pallas import tpu as pltpu
from jax.sharding import PartitionSpec as P

AXES = ("leaf", "near")
NREACH = 3
OFFSETS = (-3, -2, 2, 3)
CHIPS = 8
EARLY = 6
BF16, F32 = jnp.bfloat16, jnp.float32
VMEM = pl.BlockSpec(memory_space=pltpu.VMEM)
HBM = pl.BlockSpec(memory_space=pltpu.HBM)


def dot(a, b):
    return lax.dot_general(a, b, (((1,), (0,)), ((), ())), preferred_element_type=F32)


def dot_nt(a, b):
    return lax.dot_general(a, b, (((1,), (1,)), ((), ())), preferred_element_type=F32)


def halves(value):
    high = value.astype(BF16)
    low = (value - high.astype(F32)).astype(BF16)
    return jnp.concatenate([high, low], axis=1)


def stacked(weights, axis):
    return jnp.concatenate([w for w in weights for _ in range(2)], axis=axis)


def load(sources, targets, semaphores):
    copies = [
        pltpu.make_async_copy(source, target, semaphores.at[i])
        for i, (source, target) in enumerate(zip(sources, targets, strict=True))
    ]
    for copy in copies:
        copy.start()
    return copies


def moments_kernel(
    x_hbm, basis_hbm, transfer_hbm, level_hbm, coupling_hbm, leaf_hbm, node_hbm,
    x_ref, basis_ref, transfer_ref, chunk_ref, sibling_ref, next_ref, level_ref, coupling_ref,
    leaf_ref, node_ref, semaphores,
):
    odd = lax.axis_index("near") % 2
    copies = load(
        (x_hbm, basis_hbm, transfer_hbm, level_hbm, coupling_hbm, node_hbm, leaf_hbm),
        (x_ref, basis_ref, transfer_ref, level_ref, coupling_ref, node_ref, leaf_ref),
        semaphores,
    )
    copies[0].wait()
    copies[1].wait()
    parts = [halves(dot_nt(x_ref[j], basis_ref[j])) for j in range(4)]
    copies[2].wait()
    weights = stacked([transfer_ref[j] for j in range(4)], 0)
    moments = halves(dot(jnp.concatenate(parts, axis=1), weights))
    for j in range(chunk_ref.shape[0]):
        chunk_ref[j] = moments
    for ref, first in ((sibling_ref, 1 - odd), (next_ref, odd)):
        ref[0:3] = x_ref[pl.ds(first, 3)]
        ref[3] = jnp.concatenate(parts[:2], axis=1)
        ref[4] = jnp.concatenate(parts[2:], axis=1)
    for copy in copies[3:]:
        copy.wait()


def levels_kernel(
    nodes_ref, level_ref, coupling_ref, node_ref, even_ref, odd_ref, own_ref,
    chips, quads, octets,
):
    near = lax.axis_index("near")
    is_odd = lax.axis_index("leaf") % 2 == 1
    below = nodes_ref
    for c, table in ((0, chips), (1, quads), (2, octets)):
        count = table.shape[0]
        rows = [jnp.concatenate([below[2 * i], below[2 * i + 1]], axis=1) for i in range(count)]
        moments = halves(dot(jnp.concatenate(rows, axis=0), stacked([level_ref[c, 0], level_ref[c, 1]], 0)))
        table[...] = moments.reshape(count, 32, 128)
        below = table

    def partners(table, target, height):
        count = table.shape[0]
        node = target >> height
        parity = (near >> height) % 2
        blocks = []
        for k, offset in enumerate(OFFSETS):
            partner = node + offset
            valid = (partner >= 0) & (partner < count)
            if k == 0:
                valid = valid & (parity == 1)
            if k == 3:
                valid = valid & (parity == 0)
            block = table[jnp.clip(partner, 0, count - 1)]
            blocks.append(jnp.where(valid, block, jnp.zeros_like(block)))
        return blocks

    size = 2 * CHIPS
    targets = (near, near - size, near + size)
    rows = [
        jnp.concatenate(
            [
                block
                for c, table in ((1, chips), (2, quads), (3, octets))
                for block in partners(table, target, c)
            ],
            axis=1,
        )
        for target in targets
    ]
    down, tables = None, []
    for c in range(3):
        chosen = level_ref[c, (near >> c) % 2]
        if c == 0:
            down = chosen
        else:
            down = halves(dot(down, chosen if c == 1 else stacked([chosen], 0)))
        matrices = jnp.concatenate([coupling_ref[c, k] for k in range(4)], axis=0)
        if c == 0:
            tables.append(dot_nt(matrices, down))
        else:
            tables.append(dot_nt(jnp.concatenate([matrices, matrices], axis=1), down))
    table = halves(jnp.concatenate(tables, axis=0))
    table = stacked([table[64 * i : 64 * i + 64] for i in range(12)], 0)
    both = dot(jnp.concatenate(rows, axis=0), table)
    field = both[:, :64] + both[:, 64:]
    beside = jnp.concatenate(partners(nodes_ref, near, 0), axis=1)
    own_ref[...] = field[:32] + dot(beside, stacked([node_ref[0, k] for k in range(4)], 0))
    before = [halves(field[32:64])] + partners(nodes_ref, near - size, 0)[2:]
    after = [halves(field[64:])] + partners(nodes_ref, near + size, 0)[:2]
    for i in range(3):
        even_ref[i] = jnp.where(is_odd, before[i], after[i])
        odd_ref[i] = jnp.where(is_odd, after[i], before[i])


def near_all(window, cols, blocks, copies, near_ref, first):
    copies[4].wait()
    for j in range(4):
        total = None
        copies[j].wait()
        for k in range(7):
            place = (cols[j, k] - first) & 2047
            term = dot_nt(window[place], blocks[j, k])
            total = term if total is None else total + term
        near_ref[j] = total


def load_near(cols_hbm, blocks_hbm, cols, blocks, semaphores):
    return load(
        [blocks_hbm.at[j] for j in range(4)] + [cols_hbm],
        [blocks.at[j] for j in range(4)] + [cols],
        semaphores,
    )


def position():
    near = lax.axis_index("near")
    first = (lax.axis_index("leaf") * (2 * CHIPS) + near) * 4 - NREACH
    early = (near < EARLY) & (first + NREACH > 0)
    return near % 2 == 1, early, first


MISSING = [(j, t) for j in range(3) for t in range(j, 3)]
MISSING += [(3 - j, 9 - t) for j, t in MISSING]


def fourths(value):
    high = value.astype(BF16)
    low = (value - high.astype(F32)).astype(BF16)
    rows = [jnp.concatenate([high, high], axis=1), jnp.concatenate([low, jnp.zeros_like(low)], axis=1)]
    return jnp.concatenate(rows, axis=0)


def expand(transfer_ref, basis_ref, table_ref):
    for j in range(4):
        product = lax.dot_general(
            transfer_ref[j], basis_ref[j], (((0,), (0,)), ((), ())), preferred_element_type=F32
        )
        high = product.astype(BF16)
        columns = slice(256 * j, 256 * j + 256)
        table_ref[0:64, columns] = high
        table_ref[64:128, columns] = (product - high.astype(F32)).astype(BF16)


def early_kernel(
    x_ref, transfer_ref, basis_ref, cols_hbm, blocks_hbm,
    near_ref, rest_ref, table_ref, window, cols, blocks, semaphores,
):
    _, early, first = position()

    @pl.when(early)
    def _():
        copies = load_near(cols_hbm, blocks_hbm, cols, blocks, semaphores)
        expand(transfer_ref, basis_ref, table_ref)
        window[3:7] = x_ref[...]
        none = jnp.zeros((3, 32, 256), BF16)
        window[0:3] = none
        window[7:10] = none
        near_all(window, cols, blocks, copies, near_ref, first)
        for slot, (j, t) in enumerate(MISSING):
            k = sum(jnp.where(((cols[j, i] - first) & 2047) == t, i, 0) for i in range(7))
            rest_ref[slot] = blocks[j, k]


def near_kernel(
    x_ref, sibling_ref, next_ref, own_ref, leaf_ref, transfer_ref, basis_ref,
    begun_ref, rest_ref, early_table_ref, cols_hbm, blocks_hbm,
    near_ref, late_table_ref, window, cols, blocks, semaphores,
):
    is_odd, early, first = position()
    window[3:7] = x_ref[...]
    window[0:3] = jnp.where(is_odd, sibling_ref[0:3], next_ref[0:3])
    window[7:10] = jnp.where(is_odd, next_ref[0:3], sibling_ref[0:3])
    zero = jnp.zeros((32, 128), BF16)
    left, right = [], []
    for pair in (3, 4):
        from_sibling, from_next = sibling_ref[pair], next_ref[pair]
        before = jnp.where(is_odd, from_sibling, from_next)
        after = jnp.where(is_odd, from_next, from_sibling)
        left += [before[:, :128], before[:, 128:]]
        right += [after[:, :128], after[:, 128:]]
    rows = []
    for j in range(4):
        row = [left[j - k] if k <= j else zero for k in range(4)]
        row += [right[j + k] if k <= 3 - j else zero for k in range(4)]
        rows.append(jnp.concatenate(row, axis=1))
    matrices = stacked([leaf_ref[k] for k in range(8)], 0)
    coupled = halves(dot(jnp.concatenate(rows, axis=0), matrices))
    field = fourths(own_ref[...])

    def add_far(j, table_ref):
        leaf_part = dot(coupled[32 * j : 32 * j + 32], stacked([basis_ref[j]], 0))
        both = dot(field, table_ref[:, 256 * j : 256 * j + 256])
        return leaf_part + both[:32] + both[32:]

    @pl.when(early)
    def _():
        for j in range(4):
            total = begun_ref[j] + add_far(j, early_table_ref)
            for slot, (leaf, t) in enumerate(MISSING):
                if leaf == j:
                    total += dot_nt(window[t], rest_ref[slot])
            near_ref[j] = total

    @pl.when(jnp.logical_not(early))
    def _():
        copies = load_near(cols_hbm, blocks_hbm, cols, blocks, semaphores)
        expand(transfer_ref, basis_ref, late_table_ref)
        near_all(window, cols, blocks, copies, near_ref, first)
        for j in range(4):
            near_ref[j] += add_far(j, late_table_ref)


def product_kernel(
    near_ref, even_ref, odd_ref, node_ref, early_table_ref, late_table_ref, out_hbm, out, semaphores
):
    _, early, _ = position()
    is_odd = lax.axis_index("leaf") % 2 == 1
    given = even_ref[0].astype(F32) + odd_ref[0].astype(F32)
    row = [jnp.where(is_odd, even_ref[i], odd_ref[i]) for i in (1, 2)]
    row += [jnp.where(is_odd, odd_ref[i], even_ref[i]) for i in (1, 2)]
    beside = dot(jnp.concatenate(row, axis=1), stacked([node_ref[0, k] for k in range(4)], 0))
    field = fourths(given[:, :64] + given[:, 64:] + beside)

    def finish(table_ref):
        copies = []
        for j in range(4):
            both = dot(field, table_ref[:, 256 * j : 256 * j + 256])
            out[j] = near_ref[j] + both[:32] + both[32:]
            copies.append(pltpu.make_async_copy(out.at[j], out_hbm.at[j], semaphores.at[j]))
            copies[-1].start()
        for copy in copies:
            copy.wait()

    @pl.when(early)
    def _():
        finish(early_table_ref)

    @pl.when(jnp.logical_not(early))
    def _():
        finish(late_table_ref)


def call(kernel, out, specs, scratch=(), flops=0, size=0, out_spec=VMEM, aliases=()):
    return pl.pallas_call(
        kernel,
        out_shape=[jax.ShapeDtypeStruct(shape, dtype) for shape, dtype in out],
        in_specs=specs,
        out_specs=out_spec if isinstance(out_spec, list) else [out_spec] * len(out),
        input_output_aliases=dict(aliases),
        scratch_shapes=list(scratch),
        compiler_params=pltpu.CompilerParams(vmem_limit_bytes=16 << 20),
        cost_estimate=pl.CostEstimate(flops=flops, bytes_accessed=size, transcendentals=0),
    )


def in_hbm(*arrays):
    return [pltpu.with_memory_space_constraint(array, pltpu.HBM) for array in arrays]


def permute(value, partner):
    members = lax.axis_size(AXES)
    return lax.ppermute(value, AXES, [(i, partner(i) % members) for i in range(members)])


def local(
    input_point_values,
    leaf_cluster_basis,
    near_blocks,
    near_cols,
    leaf_transfer,
    leaf_coupling,
    node_coupling,
    level_transfer,
    level_coupling,
):
    block = lax.axis_size("near")
    x, basis, transfer, chunk, package, other_package, level, coupling, leaf, node = call(
        moments_kernel,
        [
            ((4, 32, 256), BF16),
            ((4, 64, 256), BF16),
            ((4, 64, 64), BF16),
            ((block, 32, 128), BF16),
            ((5, 32, 256), BF16),
            ((5, 32, 256), BF16),
            ((3, 2, 64, 64), BF16),
            ((3, 4, 64, 64), BF16),
            ((8, 64, 64), BF16),
            ((1, 4, 64, 64), BF16),
        ],
        [HBM] * 7,
        [pltpu.SemaphoreType.DMA((7,))],
    )(
        *in_hbm(
            input_point_values,
            leaf_cluster_basis,
            leaf_transfer,
            level_transfer,
            level_coupling,
            leaf_coupling,
            node_coupling,
        )
    )
    begun, rest, early_table = call(
        early_kernel,
        [((4, 32, 256), F32), ((12, 256, 256), BF16), ((128, 1024), BF16)],
        [VMEM] * 3 + [HBM] * 2,
        [
            pltpu.VMEM((10, 32, 256), BF16),
            pltpu.SMEM((4, 7), jnp.int32),
            pltpu.VMEM((4, 7, 256, 256), BF16),
            pltpu.SemaphoreType.DMA((5,)),
        ],
    )(x, transfer, basis, *in_hbm(near_cols, near_blocks))
    chunk, begun, package, other_package = lax.optimization_barrier(
        (chunk, begun, package, other_package)
    )
    nodes = lax.all_to_all(chunk, "near", 0, 0)
    after = permute(other_package, lambda i: i + 1 if i % 2 else i - 1)
    sibling = permute(package, lambda i: i ^ 1)
    even, odd, own = call(
        levels_kernel,
        [((3, 32, 128), BF16), ((3, 32, 128), BF16), ((32, 64), F32)],
        [VMEM] * 4,
        [
            pltpu.VMEM((8, 32, 128), BF16),
            pltpu.VMEM((4, 32, 128), BF16),
            pltpu.VMEM((2, 32, 128), BF16),
        ],
    )(nodes, level, coupling, node)
    odd = permute(odd, lambda i: i + block if i // block % 2 else i - block)
    even = permute(even, lambda i: i - block if i // block % 2 else i + block)
    near, late_table = call(
        near_kernel,
        [((4, 32, 256), F32), ((128, 1024), BF16)],
        [VMEM] * 10 + [HBM] * 2,
        [
            pltpu.VMEM((10, 32, 256), BF16),
            pltpu.SMEM((4, 7), jnp.int32),
            pltpu.VMEM((4, 7, 256, 256), BF16),
            pltpu.SemaphoreType.DMA((5,)),
        ],
        flops=200_000_000,
        size=4_000_000,
    )(
        x,
        sibling,
        after,
        own,
        leaf,
        transfer,
        basis,
        begun,
        rest,
        early_table,
        *in_hbm(near_cols, near_blocks),
    )
    (out,) = call(
        product_kernel,
        [((4, 32, 256), F32)],
        [VMEM] * 6,
        [pltpu.VMEM((4, 32, 256), F32), pltpu.SemaphoreType.DMA((4,))],
        out_spec=HBM,
    )(near, even, odd, node, early_table, late_table)
    return out


def solution(mesh):
    spread = P(AXES)
    placed = (spread, spread, spread, spread, spread, P(), spread, P(), P())
    return jax.shard_map(
        local, mesh=mesh, in_specs=placed, out_specs=spread, check_vma=False
    )
```

```python
import jax
import jax.numpy as jnp
from jax import lax
from jax.experimental import pallas as pl
from jax.experimental.pallas import tpu as pltpu
from jax.sharding import PartitionSpec as P

AXES = ("leaf", "near")
NREACH = 3
OFFSETS = (-3, -2, 2, 3)
CHIPS = 8
EARLY = 6
BF16, F32 = jnp.bfloat16, jnp.float32
VMEM = pl.BlockSpec(memory_space=pltpu.VMEM)
HBM = pl.BlockSpec(memory_space=pltpu.HBM)


def dot(a, b):
    return lax.dot_general(a, b, (((1,), (0,)), ((), ())), preferred_element_type=F32)


def dot_nt(a, b):
    return lax.dot_general(a, b, (((1,), (1,)), ((), ())), preferred_element_type=F32)


def halves(value):
    high = value.astype(BF16)
    low = (value - high.astype(F32)).astype(BF16)
    return jnp.concatenate([high, low], axis=1)


def stacked(weights, axis):
    return jnp.concatenate([w for w in weights for _ in range(2)], axis=axis)


def load(sources, targets, semaphores):
    copies = [
        pltpu.make_async_copy(source, target, semaphores.at[i])
        for i, (source, target) in enumerate(zip(sources, targets, strict=True))
    ]
    for copy in copies:
        copy.start()
    return copies


def moments_kernel(
    x_hbm, basis_hbm, transfer_hbm, level_hbm, coupling_hbm, leaf_hbm, node_hbm,
    x_ref, basis_ref, transfer_ref, chunk_hbm, sibling_ref, next_ref, level_ref, table_ref,
    leaf_ref, node_ref, coupling, chunk, semaphores,
):
    near = lax.axis_index("near")
    odd = near % 2
    copies = load(
        (x_hbm, basis_hbm, transfer_hbm, level_hbm, coupling_hbm, node_hbm, leaf_hbm),
        (x_ref, basis_ref, transfer_ref, level_ref, coupling, node_ref, leaf_ref),
        semaphores,
    )
    copies[0].wait()
    copies[1].wait()
    parts = [halves(dot_nt(x_ref[j], basis_ref[j])) for j in range(4)]
    copies[2].wait()
    weights = stacked([transfer_ref[j] for j in range(4)], 0)
    moments = halves(dot(jnp.concatenate(parts, axis=1), weights))
    for j in range(chunk.shape[0]):
        chunk[j] = moments
    send = pltpu.make_async_copy(chunk, chunk_hbm, semaphores.at[7])
    send.start()
    for copy in copies[3:]:
        copy.wait()
    down = None
    for c in range(3):
        chosen = level_ref[c, (near >> c) % 2]
        matrices = jnp.concatenate([coupling[c, k] for k in range(4)], axis=0)
        if c == 0:
            down = chosen
        else:
            down = halves(dot(down, chosen if c == 1 else stacked([chosen], 0)))
            matrices = jnp.concatenate([matrices, matrices], axis=1)
        table_ref[256 * c : 256 * c + 256] = halves(dot_nt(matrices, down))
    for ref, first in ((sibling_ref, 1 - odd), (next_ref, odd)):
        ref[0:3] = x_ref[pl.ds(first, 3)]
        ref[3] = jnp.concatenate(parts[:2], axis=1)
        ref[4] = jnp.concatenate(parts[2:], axis=1)
    send.wait()


def levels_kernel(
    nodes_ref, level_ref, table_ref, node_ref, first_ref, odd_ref, even_ref, own_ref,
    chips, quads, octets,
):
    near = lax.axis_index("near")
    is_odd = lax.axis_index("leaf") % 2 == 1
    below = nodes_ref
    for c, table in ((0, chips), (1, quads), (2, octets)):
        count = table.shape[0]
        rows = [jnp.concatenate([below[2 * i], below[2 * i + 1]], axis=1) for i in range(count)]
        moments = halves(dot(jnp.concatenate(rows, axis=0), stacked([level_ref[c, 0], level_ref[c, 1]], 0)))
        table[...] = moments.reshape(count, 32, 128)
        below = table

    def partners(table, target, height):
        count = table.shape[0]
        node = target >> height
        parity = (near >> height) % 2
        blocks = []
        for k, offset in enumerate(OFFSETS):
            partner = node + offset
            valid = (partner >= 0) & (partner < count)
            if k == 0:
                valid = valid & (parity == 1)
            if k == 3:
                valid = valid & (parity == 0)
            block = table[jnp.clip(partner, 0, count - 1)]
            blocks.append(jnp.where(valid, block, jnp.zeros_like(block)))
        return blocks

    size = 2 * CHIPS
    targets = (near, near - size, near + size)
    rows = [
        jnp.concatenate(
            [
                block
                for c, table in ((1, chips), (2, quads), (3, octets))
                for block in partners(table, target, c)
            ],
            axis=1,
        )
        for target in targets
    ]
    table = stacked([table_ref[64 * i : 64 * i + 64] for i in range(12)], 0)
    both = dot(jnp.concatenate(rows, axis=0), table)
    field = both[:, :64] + both[:, 64:]
    beside = jnp.concatenate(partners(nodes_ref, near, 0), axis=1)
    own_ref[...] = field[:32] + dot(beside, stacked([node_ref[0, k] for k in range(4)], 0))
    before = [halves(field[32:64])] + partners(nodes_ref, near - size, 0)[2:]
    after = [halves(field[64:])] + partners(nodes_ref, near + size, 0)[:2]
    for i in range(3):
        even_ref[i] = jnp.where(is_odd, before[i], after[i])
        odd_ref[i] = jnp.where(is_odd, after[i], before[i])
        first_ref[i] = before[i]
    zero = jnp.zeros((32, 128), BF16)
    odd_ref[3] = zero
    first_ref[3] = zero
    first_ref[4] = zero


def near_all(window, cols, blocks, copies, near_ref, first):
    copies[4].wait()
    for j in range(4):
        total = None
        copies[j].wait()
        for k in range(7):
            place = (cols[j, k] - first) & 2047
            term = dot_nt(window[place], blocks[j, k])
            total = term if total is None else total + term
        near_ref[j] = total


def load_near(cols_hbm, blocks_hbm, cols, blocks, semaphores):
    return load(
        [blocks_hbm.at[j] for j in range(4)] + [cols_hbm],
        [blocks.at[j] for j in range(4)] + [cols],
        semaphores,
    )


def position():
    near = lax.axis_index("near")
    first = (lax.axis_index("leaf") * (2 * CHIPS) + near) * 4 - NREACH
    early = (near < EARLY) & (first + NREACH > 0)
    return near % 2 == 1, early, first


MISSING = [(j, t) for j in range(3) for t in range(j, 3)]
MISSING += [(3 - j, 9 - t) for j, t in MISSING]


def fourths(value):
    high = value.astype(BF16)
    low = (value - high.astype(F32)).astype(BF16)
    rows = [jnp.concatenate([high, high], axis=1), jnp.concatenate([low, jnp.zeros_like(low)], axis=1)]
    return jnp.concatenate(rows, axis=0)


def expand(transfer_ref, basis_ref, table_ref):
    for j in range(4):
        product = lax.dot_general(
            transfer_ref[j], basis_ref[j], (((0,), (0,)), ((), ())), preferred_element_type=F32
        )
        high = product.astype(BF16)
        columns = slice(256 * j, 256 * j + 256)
        table_ref[0:64, columns] = high
        table_ref[64:128, columns] = (product - high.astype(F32)).astype(BF16)


def early_kernel(
    x_ref, transfer_ref, basis_ref, cols_hbm, blocks_hbm,
    near_ref, rest_ref, table_ref, window, cols, blocks, semaphores,
):
    _, early, first = position()

    @pl.when(early)
    def _():
        copies = load_near(cols_hbm, blocks_hbm, cols, blocks, semaphores)
        expand(transfer_ref, basis_ref, table_ref)
        window[3:7] = x_ref[...]
        none = jnp.zeros((3, 32, 256), BF16)
        window[0:3] = none
        window[7:10] = none
        near_all(window, cols, blocks, copies, near_ref, first)
        for slot, (j, t) in enumerate(MISSING):
            k = sum(jnp.where(((cols[j, i] - first) & 2047) == t, i, 0) for i in range(7))
            rest_ref[slot] = blocks[j, k]


def near_kernel(
    x_ref, sibling_ref, next_ref, own_ref, leaf_ref, transfer_ref, basis_ref,
    begun_ref, rest_ref, early_table_ref, cols_hbm, blocks_hbm,
    near_ref, late_table_ref, window, cols, blocks, semaphores,
):
    is_odd, early, first = position()
    window[3:7] = x_ref[...]
    window[0:3] = jnp.where(is_odd, sibling_ref[0:3], next_ref[0:3])
    window[7:10] = jnp.where(is_odd, next_ref[0:3], sibling_ref[0:3])
    zero = jnp.zeros((32, 128), BF16)
    left, right = [], []
    for pair in (3, 4):
        from_sibling, from_next = sibling_ref[pair], next_ref[pair]
        before = jnp.where(is_odd, from_sibling, from_next)
        after = jnp.where(is_odd, from_next, from_sibling)
        left += [before[:, :128], before[:, 128:]]
        right += [after[:, :128], after[:, 128:]]
    rows = []
    for j in range(4):
        row = [left[j - k] if k <= j else zero for k in range(4)]
        row += [right[j + k] if k <= 3 - j else zero for k in range(4)]
        rows.append(jnp.concatenate(row, axis=1))
    matrices = stacked([leaf_ref[k] for k in range(8)], 0)
    coupled = halves(dot(jnp.concatenate(rows, axis=0), matrices))
    field = fourths(own_ref[...])

    def add_far(j, table_ref):
        leaf_part = dot(coupled[32 * j : 32 * j + 32], stacked([basis_ref[j]], 0))
        both = dot(field, table_ref[:, 256 * j : 256 * j + 256])
        return leaf_part + both[:32] + both[32:]

    @pl.when(early)
    def _():
        for j in range(4):
            total = begun_ref[j] + add_far(j, early_table_ref)
            for slot, (leaf, t) in enumerate(MISSING):
                if leaf == j:
                    total += dot_nt(window[t], rest_ref[slot])
            near_ref[j] = total

    @pl.when(jnp.logical_not(early))
    def _():
        copies = load_near(cols_hbm, blocks_hbm, cols, blocks, semaphores)
        expand(transfer_ref, basis_ref, late_table_ref)
        near_all(window, cols, blocks, copies, near_ref, first)
        for j in range(4):
            near_ref[j] += add_far(j, late_table_ref)


def product_kernel(
    near_ref, first_ref, odd_ref, even_ref, node_ref, early_table_ref, late_table_ref, out_hbm,
    out, semaphores,
):
    _, early, _ = position()
    is_odd = lax.axis_index("leaf") % 2 == 1
    even = [first_ref[i] + even_ref[i] for i in range(3)]
    given = even[0].astype(F32) + odd_ref[0].astype(F32)
    row = [jnp.where(is_odd, even[i], odd_ref[i]) for i in (1, 2)]
    row += [jnp.where(is_odd, odd_ref[i], even[i]) for i in (1, 2)]
    beside = dot(jnp.concatenate(row, axis=1), stacked([node_ref[0, k] for k in range(4)], 0))
    field = fourths(given[:, :64] + given[:, 64:] + beside)

    def finish(table_ref):
        copies = []
        for j in range(4):
            both = dot(field, table_ref[:, 256 * j : 256 * j + 256])
            out[j] = near_ref[j] + both[:32] + both[32:]
            copies.append(pltpu.make_async_copy(out.at[j], out_hbm.at[j], semaphores.at[j]))
            copies[-1].start()
        for copy in copies:
            copy.wait()

    @pl.when(early)
    def _():
        finish(early_table_ref)

    @pl.when(jnp.logical_not(early))
    def _():
        finish(late_table_ref)


def call(kernel, out, specs, scratch=(), flops=0, size=0, out_spec=VMEM, aliases=()):
    return pl.pallas_call(
        kernel,
        out_shape=[jax.ShapeDtypeStruct(shape, dtype) for shape, dtype in out],
        in_specs=specs,
        out_specs=out_spec if isinstance(out_spec, list) else [out_spec] * len(out),
        input_output_aliases=dict(aliases),
        scratch_shapes=list(scratch),
        compiler_params=pltpu.CompilerParams(vmem_limit_bytes=16 << 20),
        cost_estimate=pl.CostEstimate(flops=flops, bytes_accessed=size, transcendentals=0),
    )


def in_hbm(*arrays):
    return [pltpu.with_memory_space_constraint(array, pltpu.HBM) for array in arrays]


def permute(value, partner, taking=lambda i: True):
    members = lax.axis_size(AXES)
    pairs = [(i, partner(i) % members) for i in range(members) if taking(i)]
    return lax.ppermute(value, AXES, pairs)


def local(
    input_point_values,
    leaf_cluster_basis,
    near_blocks,
    near_cols,
    leaf_transfer,
    leaf_coupling,
    node_coupling,
    level_transfer,
    level_coupling,
):
    block = lax.axis_size("near")
    x, basis, transfer, chunk, package, other_package, level, coupling, leaf, node = call(
        moments_kernel,
        [
            ((4, 32, 256), BF16),
            ((4, 64, 256), BF16),
            ((4, 64, 64), BF16),
            ((block, 32, 128), BF16),
            ((5, 32, 256), BF16),
            ((5, 32, 256), BF16),
            ((3, 2, 64, 64), BF16),
            ((768, 128), BF16),
            ((8, 64, 64), BF16),
            ((1, 4, 64, 64), BF16),
        ],
        [HBM] * 7,
        [
            pltpu.VMEM((3, 4, 64, 64), BF16),
            pltpu.VMEM((block, 32, 128), BF16),
            pltpu.SemaphoreType.DMA((8,)),
        ],
        out_spec=[VMEM] * 3 + [HBM] + [VMEM] * 6,
    )(
        *in_hbm(
            input_point_values,
            leaf_cluster_basis,
            leaf_transfer,
            level_transfer,
            level_coupling,
            leaf_coupling,
            node_coupling,
        )
    )
    begun, rest, early_table = call(
        early_kernel,
        [((4, 32, 256), F32), ((12, 256, 256), BF16), ((128, 1024), BF16)],
        [VMEM] * 3 + [HBM] * 2,
        [
            pltpu.VMEM((10, 32, 256), BF16),
            pltpu.SMEM((4, 7), jnp.int32),
            pltpu.VMEM((4, 7, 256, 256), BF16),
            pltpu.SemaphoreType.DMA((5,)),
        ],
    )(x, transfer, basis, *in_hbm(near_cols, near_blocks))
    chunk, begun, package, other_package = lax.optimization_barrier(
        (chunk, begun, package, other_package)
    )
    nodes = lax.all_to_all(chunk, "near", 0, 0)
    after = permute(other_package, lambda i: i + 1 if i % 2 else i - 1)
    sibling = permute(package, lambda i: i ^ 1)
    first, odd, even, own = call(
        levels_kernel,
        [((5, 32, 128), BF16), ((4, 32, 128), BF16), ((3, 32, 128), BF16), ((32, 64), F32)],
        [VMEM] * 4,
        [
            pltpu.VMEM((8, 32, 128), BF16),
            pltpu.VMEM((4, 32, 128), BF16),
            pltpu.VMEM((2, 32, 128), BF16),
        ],
    )(nodes, level, coupling, node)

    def to_first(i):
        return i // block == 1 and i % block > 0

    first = permute(first, lambda i: i - block, to_first)
    odd = permute(odd, lambda i: i + block if i // block % 2 else i - block)
    even = permute(
        even, lambda i: i - block if i // block % 2 else i + block, lambda i: not to_first(i)
    )
    near, late_table = call(
        near_kernel,
        [((4, 32, 256), F32), ((128, 1024), BF16)],
        [VMEM] * 10 + [HBM] * 2,
        [
            pltpu.VMEM((10, 32, 256), BF16),
            pltpu.SMEM((4, 7), jnp.int32),
            pltpu.VMEM((4, 7, 256, 256), BF16),
            pltpu.SemaphoreType.DMA((5,)),
        ],
        flops=200_000_000,
        size=4_000_000,
    )(
        x,
        sibling,
        after,
        own,
        leaf,
        transfer,
        basis,
        begun,
        rest,
        early_table,
        *in_hbm(near_cols, near_blocks),
    )
    (out,) = call(
        product_kernel,
        [((4, 32, 256), F32)],
        [VMEM] * 7,
        [pltpu.VMEM((4, 32, 256), F32), pltpu.SemaphoreType.DMA((4,))],
        out_spec=HBM,
    )(near, first, odd, even, node, early_table, late_table)
    return out


def solution(mesh):
    spread = P(AXES)
    placed = (spread, spread, spread, spread, spread, P(), spread, P(), P())
    return jax.shard_map(
        local, mesh=mesh, in_specs=placed, out_specs=spread, check_vma=False
    )
```

```python
import jax
import jax.numpy as jnp
from jax import lax
from jax.experimental import pallas as pl
from jax.experimental.pallas import tpu as pltpu
from jax.sharding import PartitionSpec as P

AXES = ("leaf", "near")
NREACH = 3
OFFSETS = (-3, -2, 2, 3)
CHIPS = 8
EARLY = 6
BF16, F32 = jnp.bfloat16, jnp.float32
VMEM = pl.BlockSpec(memory_space=pltpu.VMEM)
HBM = pl.BlockSpec(memory_space=pltpu.HBM)


def dot(a, b):
    return lax.dot_general(a, b, (((1,), (0,)), ((), ())), preferred_element_type=F32)


def dot_nt(a, b):
    return lax.dot_general(a, b, (((1,), (1,)), ((), ())), preferred_element_type=F32)


def halves(value):
    high = value.astype(BF16)
    low = (value - high.astype(F32)).astype(BF16)
    return jnp.concatenate([high, low], axis=1)


def stacked(weights, axis):
    return jnp.concatenate([w for w in weights for _ in range(2)], axis=axis)


def load(sources, targets, semaphores):
    copies = [
        pltpu.make_async_copy(source, target, semaphores.at[i])
        for i, (source, target) in enumerate(zip(sources, targets, strict=True))
    ]
    for copy in copies:
        copy.start()
    return copies


def moments_kernel(
    x_hbm, basis_hbm, transfer_hbm, level_hbm, coupling_hbm, leaf_hbm, node_hbm,
    x_ref, basis_ref, transfer_ref, chunk_hbm, sibling_ref, next_ref, level_ref, table_ref,
    leaf_ref, node_ref, coupling, chunk, semaphores,
):
    near = lax.axis_index("near")
    odd = near % 2
    copies = load(
        (x_hbm, basis_hbm, transfer_hbm, level_hbm, coupling_hbm, node_hbm, leaf_hbm),
        (x_ref, basis_ref, transfer_ref, level_ref, coupling, node_ref, leaf_ref),
        semaphores,
    )
    copies[0].wait()
    copies[1].wait()
    parts = [halves(dot_nt(x_ref[j], basis_ref[j])) for j in range(4)]
    copies[2].wait()
    weights = stacked([transfer_ref[j] for j in range(4)], 0)
    moments = halves(dot(jnp.concatenate(parts, axis=1), weights))
    for j in range(chunk.shape[0]):
        chunk[j] = moments
    send = pltpu.make_async_copy(chunk, chunk_hbm, semaphores.at[7])
    send.start()
    for copy in copies[3:]:
        copy.wait()
    down = None
    for c in range(3):
        chosen = level_ref[c, (near >> c) % 2]
        matrices = jnp.concatenate([coupling[c, k] for k in range(4)], axis=0)
        if c == 0:
            down = chosen
        else:
            down = halves(dot(down, chosen if c == 1 else stacked([chosen], 0)))
            matrices = jnp.concatenate([matrices, matrices], axis=1)
        table_ref[256 * c : 256 * c + 256] = halves(dot_nt(matrices, down))
    for ref, first in ((sibling_ref, 1 - odd), (next_ref, odd)):
        ref[0:3] = x_ref[pl.ds(first, 3)]
        ref[3] = jnp.concatenate(parts[:2], axis=1)
        ref[4] = jnp.concatenate(parts[2:], axis=1)
    send.wait()


def levels_kernel(
    nodes_ref, level_ref, table_ref, node_ref, first_ref, odd_ref, even_ref, own_ref,
    chips, quads, octets,
):
    near = lax.axis_index("near")
    is_odd = lax.axis_index("leaf") % 2 == 1
    below = nodes_ref
    for c, table in ((0, chips), (1, quads), (2, octets)):
        count = table.shape[0]
        rows = [jnp.concatenate([below[2 * i], below[2 * i + 1]], axis=1) for i in range(count)]
        moments = halves(dot(jnp.concatenate(rows, axis=0), stacked([level_ref[c, 0], level_ref[c, 1]], 0)))
        table[...] = moments.reshape(count, 32, 128)
        below = table

    def partners(table, target, height):
        count = table.shape[0]
        node = target >> height
        parity = (near >> height) % 2
        blocks = []
        for k, offset in enumerate(OFFSETS):
            partner = node + offset
            valid = (partner >= 0) & (partner < count)
            if k == 0:
                valid = valid & (parity == 1)
            if k == 3:
                valid = valid & (parity == 0)
            block = table[jnp.clip(partner, 0, count - 1)]
            blocks.append(jnp.where(valid, block, jnp.zeros_like(block)))
        return blocks

    size = 2 * CHIPS
    targets = (near, near - size, near + size)
    rows = [
        jnp.concatenate(
            [
                block
                for c, table in ((1, chips), (2, quads), (3, octets))
                for block in partners(table, target, c)
            ],
            axis=1,
        )
        for target in targets
    ]
    table = stacked([table_ref[64 * i : 64 * i + 64] for i in range(12)], 0)
    both = dot(jnp.concatenate(rows, axis=0), table)
    field = both[:, :64] + both[:, 64:]
    beside = jnp.concatenate(partners(nodes_ref, near, 0), axis=1)
    own_ref[...] = field[:32] + dot(beside, stacked([node_ref[0, k] for k in range(4)], 0))
    before = [halves(field[32:64])] + partners(nodes_ref, near - size, 0)[2:]
    after = [halves(field[64:])] + partners(nodes_ref, near + size, 0)[:2]
    for i in range(3):
        even_ref[i] = jnp.where(is_odd, before[i], after[i])
        odd_ref[i] = jnp.where(is_odd, after[i], before[i])
        first_ref[i] = jnp.where(is_odd, before[i], after[i])


def near_all(window, cols, blocks, copies, near_ref, first):
    copies[4].wait()
    for j in range(4):
        total = None
        copies[j].wait()
        for k in range(7):
            place = (cols[j, k] - first) & 2047
            term = dot_nt(window[place], blocks[j, k])
            total = term if total is None else total + term
        near_ref[j] = total


def load_near(cols_hbm, blocks_hbm, cols, blocks, semaphores):
    return load(
        [blocks_hbm.at[j] for j in range(4)] + [cols_hbm],
        [blocks.at[j] for j in range(4)] + [cols],
        semaphores,
    )


def position():
    near = lax.axis_index("near")
    first = (lax.axis_index("leaf") * (2 * CHIPS) + near) * 4 - NREACH
    early = (near < EARLY) & (first + NREACH > 0)
    return near % 2 == 1, early, first


MISSING = [(j, t) for j in range(3) for t in range(j, 3)]
MISSING += [(3 - j, 9 - t) for j, t in MISSING]


def fourths(value):
    high = value.astype(BF16)
    low = (value - high.astype(F32)).astype(BF16)
    rows = [jnp.concatenate([high, high], axis=1), jnp.concatenate([low, jnp.zeros_like(low)], axis=1)]
    return jnp.concatenate(rows, axis=0)


def expand(transfer_ref, basis_ref, table_ref):
    for j in range(4):
        product = lax.dot_general(
            transfer_ref[j], basis_ref[j], (((0,), (0,)), ((), ())), preferred_element_type=F32
        )
        high = product.astype(BF16)
        columns = slice(256 * j, 256 * j + 256)
        table_ref[0:64, columns] = high
        table_ref[64:128, columns] = (product - high.astype(F32)).astype(BF16)


def early_kernel(
    x_ref, transfer_ref, basis_ref, cols_hbm, blocks_hbm,
    near_ref, rest_ref, table_ref, window, cols, blocks, semaphores,
):
    _, early, first = position()

    @pl.when(early)
    def _():
        copies = load_near(cols_hbm, blocks_hbm, cols, blocks, semaphores)
        expand(transfer_ref, basis_ref, table_ref)
        window[3:7] = x_ref[...]
        none = jnp.zeros((3, 32, 256), BF16)
        window[0:3] = none
        window[7:10] = none
        near_all(window, cols, blocks, copies, near_ref, first)
        for slot, (j, t) in enumerate(MISSING):
            k = sum(jnp.where(((cols[j, i] - first) & 2047) == t, i, 0) for i in range(7))
            rest_ref[slot] = blocks[j, k]


def near_kernel(
    x_ref, sibling_ref, next_ref, own_ref, leaf_ref, transfer_ref, basis_ref,
    begun_ref, rest_ref, early_table_ref, cols_hbm, blocks_hbm,
    near_ref, late_table_ref, window, cols, blocks, semaphores,
):
    is_odd, early, first = position()
    window[3:7] = x_ref[...]
    window[0:3] = jnp.where(is_odd, sibling_ref[0:3], next_ref[0:3])
    window[7:10] = jnp.where(is_odd, next_ref[0:3], sibling_ref[0:3])
    zero = jnp.zeros((32, 128), BF16)
    left, right = [], []
    for pair in (3, 4):
        from_sibling, from_next = sibling_ref[pair], next_ref[pair]
        before = jnp.where(is_odd, from_sibling, from_next)
        after = jnp.where(is_odd, from_next, from_sibling)
        left += [before[:, :128], before[:, 128:]]
        right += [after[:, :128], after[:, 128:]]
    rows = []
    for j in range(4):
        row = [left[j - k] if k <= j else zero for k in range(4)]
        row += [right[j + k] if k <= 3 - j else zero for k in range(4)]
        rows.append(jnp.concatenate(row, axis=1))
    matrices = stacked([leaf_ref[k] for k in range(8)], 0)
    coupled = halves(dot(jnp.concatenate(rows, axis=0), matrices))
    field = fourths(own_ref[...])

    def add_far(j, table_ref):
        leaf_part = dot(coupled[32 * j : 32 * j + 32], stacked([basis_ref[j]], 0))
        both = dot(field, table_ref[:, 256 * j : 256 * j + 256])
        return leaf_part + both[:32] + both[32:]

    @pl.when(early)
    def _():
        for j in range(4):
            total = begun_ref[j] + add_far(j, early_table_ref)
            for slot, (leaf, t) in enumerate(MISSING):
                if leaf == j:
                    total += dot_nt(window[t], rest_ref[slot])
            near_ref[j] = total

    @pl.when(jnp.logical_not(early))
    def _():
        copies = load_near(cols_hbm, blocks_hbm, cols, blocks, semaphores)
        expand(transfer_ref, basis_ref, late_table_ref)
        near_all(window, cols, blocks, copies, near_ref, first)
        for j in range(4):
            near_ref[j] += add_far(j, late_table_ref)


def product_kernel(
    near_ref, first_ref, odd_ref, even_ref, node_ref, early_table_ref, late_table_ref, out_hbm,
    out, semaphores,
):
    _, early, _ = position()
    is_odd = lax.axis_index("leaf") % 2 == 1
    even = [first_ref[i] + even_ref[i] for i in range(3)]
    given = even[0].astype(F32) + odd_ref[0].astype(F32)
    row = [jnp.where(is_odd, even[i], odd_ref[i]) for i in (1, 2)]
    row += [jnp.where(is_odd, odd_ref[i], even[i]) for i in (1, 2)]
    beside = dot(jnp.concatenate(row, axis=1), stacked([node_ref[0, k] for k in range(4)], 0))
    field = fourths(given[:, :64] + given[:, 64:] + beside)

    def finish(table_ref):
        copies = []
        for j in range(4):
            both = dot(field, table_ref[:, 256 * j : 256 * j + 256])
            out[j] = near_ref[j] + both[:32] + both[32:]
            copies.append(pltpu.make_async_copy(out.at[j], out_hbm.at[j], semaphores.at[j]))
            copies[-1].start()
        for copy in copies:
            copy.wait()

    @pl.when(early)
    def _():
        finish(early_table_ref)

    @pl.when(jnp.logical_not(early))
    def _():
        finish(late_table_ref)


def call(kernel, out, specs, scratch=(), flops=0, size=0, out_spec=VMEM, aliases=()):
    return pl.pallas_call(
        kernel,
        out_shape=[jax.ShapeDtypeStruct(shape, dtype) for shape, dtype in out],
        in_specs=specs,
        out_specs=out_spec if isinstance(out_spec, list) else [out_spec] * len(out),
        input_output_aliases=dict(aliases),
        scratch_shapes=list(scratch),
        compiler_params=pltpu.CompilerParams(vmem_limit_bytes=16 << 20),
        cost_estimate=pl.CostEstimate(flops=flops, bytes_accessed=size, transcendentals=0),
    )


def in_hbm(*arrays):
    return [pltpu.with_memory_space_constraint(array, pltpu.HBM) for array in arrays]


def permute(value, partner, taking=lambda i: True):
    members = lax.axis_size(AXES)
    pairs = [(i, partner(i) % members) for i in range(members) if taking(i)]
    return lax.ppermute(value, AXES, pairs)


def local(
    input_point_values,
    leaf_cluster_basis,
    near_blocks,
    near_cols,
    leaf_transfer,
    leaf_coupling,
    node_coupling,
    level_transfer,
    level_coupling,
):
    block = lax.axis_size("near")
    x, basis, transfer, chunk, package, other_package, level, coupling, leaf, node = call(
        moments_kernel,
        [
            ((4, 32, 256), BF16),
            ((4, 64, 256), BF16),
            ((4, 64, 64), BF16),
            ((block, 32, 128), BF16),
            ((5, 32, 256), BF16),
            ((5, 32, 256), BF16),
            ((3, 2, 64, 64), BF16),
            ((768, 128), BF16),
            ((8, 64, 64), BF16),
            ((1, 4, 64, 64), BF16),
        ],
        [HBM] * 7,
        [
            pltpu.VMEM((3, 4, 64, 64), BF16),
            pltpu.VMEM((block, 32, 128), BF16),
            pltpu.SemaphoreType.DMA((8,)),
        ],
        out_spec=[VMEM] * 3 + [HBM] + [VMEM] * 6,
    )(
        *in_hbm(
            input_point_values,
            leaf_cluster_basis,
            leaf_transfer,
            level_transfer,
            level_coupling,
            leaf_coupling,
            node_coupling,
        )
    )
    begun, rest, early_table = call(
        early_kernel,
        [((4, 32, 256), F32), ((12, 256, 256), BF16), ((128, 1024), BF16)],
        [VMEM] * 3 + [HBM] * 2,
        [
            pltpu.VMEM((10, 32, 256), BF16),
            pltpu.SMEM((4, 7), jnp.int32),
            pltpu.VMEM((4, 7, 256, 256), BF16),
            pltpu.SemaphoreType.DMA((5,)),
        ],
    )(x, transfer, basis, *in_hbm(near_cols, near_blocks))
    chunk, begun, package, other_package = lax.optimization_barrier(
        (chunk, begun, package, other_package)
    )
    nodes = lax.all_to_all(chunk, "near", 0, 0)
    after = permute(other_package, lambda i: i + 1 if i % 2 else i - 1)
    sibling = permute(package, lambda i: i ^ 1)
    first, odd, even, own = call(
        levels_kernel,
        [((3, 32, 128), BF16), ((3, 32, 128), BF16), ((3, 32, 128), BF16), ((32, 64), F32)],
        [VMEM] * 4,
        [
            pltpu.VMEM((8, 32, 128), BF16),
            pltpu.VMEM((4, 32, 128), BF16),
            pltpu.VMEM((2, 32, 128), BF16),
        ],
    )(nodes, level, coupling, node)

    def to_first(i):
        return i // block == 1 and i % block > 0 or i == 0

    first = permute(first, lambda i: i - block if i // block % 2 else i + block, to_first)
    odd = permute(odd, lambda i: i + block if i // block % 2 else i - block)
    even = permute(
        even, lambda i: i - block if i // block % 2 else i + block, lambda i: not to_first(i)
    )
    near, late_table = call(
        near_kernel,
        [((4, 32, 256), F32), ((128, 1024), BF16)],
        [VMEM] * 10 + [HBM] * 2,
        [
            pltpu.VMEM((10, 32, 256), BF16),
            pltpu.SMEM((4, 7), jnp.int32),
            pltpu.VMEM((4, 7, 256, 256), BF16),
            pltpu.SemaphoreType.DMA((5,)),
        ],
        flops=200_000_000,
        size=4_000_000,
    )(
        x,
        sibling,
        after,
        own,
        leaf,
        transfer,
        basis,
        begun,
        rest,
        early_table,
        *in_hbm(near_cols, near_blocks),
    )
    (out,) = call(
        product_kernel,
        [((4, 32, 256), F32)],
        [VMEM] * 7,
        [pltpu.VMEM((4, 32, 256), F32), pltpu.SemaphoreType.DMA((4,))],
        out_spec=HBM,
    )(near, first, odd, even, node, early_table, late_table)
    return out


def solution(mesh):
    spread = P(AXES)
    placed = (spread, spread, spread, spread, spread, P(), spread, P(), P())
    return jax.shard_map(
        local, mesh=mesh, in_specs=placed, out_specs=spread, check_vma=False
    )
```

```python
import jax
import jax.numpy as jnp
from jax import lax
from jax.experimental import pallas as pl
from jax.experimental.pallas import tpu as pltpu
from jax.sharding import PartitionSpec as P

AXES = ("leaf", "near")
NREACH = 3
OFFSETS = (-3, -2, 2, 3)
CHIPS = 8
EARLY = 6
BF16, F32 = jnp.bfloat16, jnp.float32
VMEM = pl.BlockSpec(memory_space=pltpu.VMEM)
HBM = pl.BlockSpec(memory_space=pltpu.HBM)


def dot(a, b):
    return lax.dot_general(a, b, (((1,), (0,)), ((), ())), preferred_element_type=F32)


def dot_nt(a, b):
    return lax.dot_general(a, b, (((1,), (1,)), ((), ())), preferred_element_type=F32)


def halves(value):
    high = value.astype(BF16)
    low = (value - high.astype(F32)).astype(BF16)
    return jnp.concatenate([high, low], axis=1)


def stacked(weights, axis):
    return jnp.concatenate([w for w in weights for _ in range(2)], axis=axis)


def load(sources, targets, semaphores):
    copies = [
        pltpu.make_async_copy(source, target, semaphores.at[i])
        for i, (source, target) in enumerate(zip(sources, targets, strict=True))
    ]
    for copy in copies:
        copy.start()
    return copies


def moments_kernel(
    x_hbm, basis_hbm, transfer_hbm, level_hbm, coupling_hbm, leaf_hbm, node_hbm,
    x_ref, basis_ref, transfer_ref, chunk_hbm, sibling_ref, next_ref, level_ref, table_ref,
    leaf_ref, node_ref, coupling, chunk, semaphores,
):
    near = lax.axis_index("near")
    odd = near % 2
    copies = load(
        (x_hbm, basis_hbm, transfer_hbm), (x_ref, basis_ref, transfer_ref), semaphores
    )
    copies[0].wait()
    copies[1].wait()
    copies += load(
        (level_hbm, coupling_hbm, node_hbm, leaf_hbm),
        (level_ref, coupling, node_ref, leaf_ref),
        semaphores.at[pl.ds(3, 4)],
    )
    parts = [halves(dot_nt(x_ref[j], basis_ref[j])) for j in range(4)]
    copies[2].wait()
    weights = stacked([transfer_ref[j] for j in range(4)], 0)
    moments = halves(dot(jnp.concatenate(parts, axis=1), weights))
    for j in range(chunk.shape[0]):
        chunk[j] = moments
    send = pltpu.make_async_copy(chunk, chunk_hbm, semaphores.at[7])
    send.start()
    for copy in copies[3:]:
        copy.wait()
    down = None
    for c in range(3):
        chosen = level_ref[c, (near >> c) % 2]
        matrices = jnp.concatenate([coupling[c, k] for k in range(4)], axis=0)
        if c == 0:
            down = chosen
        else:
            down = halves(dot(down, chosen if c == 1 else stacked([chosen], 0)))
            matrices = jnp.concatenate([matrices, matrices], axis=1)
        table_ref[256 * c : 256 * c + 256] = halves(dot_nt(matrices, down))
    for ref, first in ((sibling_ref, 1 - odd), (next_ref, odd)):
        ref[0:3] = x_ref[pl.ds(first, 3)]
        ref[3] = jnp.concatenate(parts[:2], axis=1)
        ref[4] = jnp.concatenate(parts[2:], axis=1)
    send.wait()


def levels_kernel(
    nodes_ref, level_ref, table_ref, node_ref, first_ref, odd_ref, even_ref, own_ref,
    chips, quads, octets,
):
    near = lax.axis_index("near")
    is_odd = lax.axis_index("leaf") % 2 == 1
    below = nodes_ref
    for c, table in ((0, chips), (1, quads), (2, octets)):
        count = table.shape[0]
        rows = [jnp.concatenate([below[2 * i], below[2 * i + 1]], axis=1) for i in range(count)]
        moments = halves(dot(jnp.concatenate(rows, axis=0), stacked([level_ref[c, 0], level_ref[c, 1]], 0)))
        table[...] = moments.reshape(count, 32, 128)
        below = table

    def partners(table, target, height):
        count = table.shape[0]
        node = target >> height
        parity = (near >> height) % 2
        blocks = []
        for k, offset in enumerate(OFFSETS):
            partner = node + offset
            valid = (partner >= 0) & (partner < count)
            if k == 0:
                valid = valid & (parity == 1)
            if k == 3:
                valid = valid & (parity == 0)
            block = table[jnp.clip(partner, 0, count - 1)]
            blocks.append(jnp.where(valid, block, jnp.zeros_like(block)))
        return blocks

    size = 2 * CHIPS
    targets = (near, near - size, near + size)
    rows = [
        jnp.concatenate(
            [
                block
                for c, table in ((1, chips), (2, quads), (3, octets))
                for block in partners(table, target, c)
            ],
            axis=1,
        )
        for target in targets
    ]
    table = stacked([table_ref[64 * i : 64 * i + 64] for i in range(12)], 0)
    both = dot(jnp.concatenate(rows, axis=0), table)
    field = both[:, :64] + both[:, 64:]
    beside = jnp.concatenate(partners(nodes_ref, near, 0), axis=1)
    own_ref[...] = field[:32] + dot(beside, stacked([node_ref[0, k] for k in range(4)], 0))
    before = [halves(field[32:64])] + partners(nodes_ref, near - size, 0)[2:]
    after = [halves(field[64:])] + partners(nodes_ref, near + size, 0)[:2]
    for i in range(3):
        even_ref[i] = jnp.where(is_odd, before[i], after[i])
        odd_ref[i] = jnp.where(is_odd, after[i], before[i])
        first_ref[i] = jnp.where(is_odd, before[i], after[i])


def near_all(window, cols, blocks, copies, near_ref, first):
    copies[4].wait()
    for j in range(4):
        total = None
        copies[j].wait()
        for k in range(7):
            place = (cols[j, k] - first) & 2047
            term = dot_nt(window[place], blocks[j, k])
            total = term if total is None else total + term
        near_ref[j] = total


def load_near(cols_hbm, blocks_hbm, cols, blocks, semaphores):
    return load(
        [blocks_hbm.at[j] for j in range(4)] + [cols_hbm],
        [blocks.at[j] for j in range(4)] + [cols],
        semaphores,
    )


def position():
    near = lax.axis_index("near")
    first = (lax.axis_index("leaf") * (2 * CHIPS) + near) * 4 - NREACH
    early = (near < EARLY) & (first + NREACH > 0)
    return near % 2 == 1, early, first


MISSING = [(j, t) for j in range(3) for t in range(j, 3)]
MISSING += [(3 - j, 9 - t) for j, t in MISSING]


def fourths(value):
    high = value.astype(BF16)
    low = (value - high.astype(F32)).astype(BF16)
    rows = [jnp.concatenate([high, high], axis=1), jnp.concatenate([low, jnp.zeros_like(low)], axis=1)]
    return jnp.concatenate(rows, axis=0)


def expand(transfer_ref, basis_ref, table_ref):
    for j in range(4):
        product = lax.dot_general(
            transfer_ref[j], basis_ref[j], (((0,), (0,)), ((), ())), preferred_element_type=F32
        )
        high = product.astype(BF16)
        columns = slice(256 * j, 256 * j + 256)
        table_ref[0:64, columns] = high
        table_ref[64:128, columns] = (product - high.astype(F32)).astype(BF16)


def early_kernel(
    x_ref, transfer_ref, basis_ref, cols_hbm, blocks_hbm,
    near_ref, rest_ref, table_ref, window, cols, blocks, semaphores,
):
    _, early, first = position()

    @pl.when(early)
    def _():
        copies = load_near(cols_hbm, blocks_hbm, cols, blocks, semaphores)
        expand(transfer_ref, basis_ref, table_ref)
        window[3:7] = x_ref[...]
        none = jnp.zeros((3, 32, 256), BF16)
        window[0:3] = none
        window[7:10] = none
        near_all(window, cols, blocks, copies, near_ref, first)
        for slot, (j, t) in enumerate(MISSING):
            k = sum(jnp.where(((cols[j, i] - first) & 2047) == t, i, 0) for i in range(7))
            rest_ref[slot] = blocks[j, k]


def near_kernel(
    x_ref, sibling_ref, next_ref, own_ref, leaf_ref, transfer_ref, basis_ref,
    begun_ref, rest_ref, early_table_ref, cols_hbm, blocks_hbm,
    near_ref, late_table_ref, window, cols, blocks, semaphores,
):
    is_odd, early, first = position()
    window[3:7] = x_ref[...]
    window[0:3] = jnp.where(is_odd, sibling_ref[0:3], next_ref[0:3])
    window[7:10] = jnp.where(is_odd, next_ref[0:3], sibling_ref[0:3])
    zero = jnp.zeros((32, 128), BF16)
    left, right = [], []
    for pair in (3, 4):
        from_sibling, from_next = sibling_ref[pair], next_ref[pair]
        before = jnp.where(is_odd, from_sibling, from_next)
        after = jnp.where(is_odd, from_next, from_sibling)
        left += [before[:, :128], before[:, 128:]]
        right += [after[:, :128], after[:, 128:]]
    rows = []
    for j in range(4):
        row = [left[j - k] if k <= j else zero for k in range(4)]
        row += [right[j + k] if k <= 3 - j else zero for k in range(4)]
        rows.append(jnp.concatenate(row, axis=1))
    matrices = stacked([leaf_ref[k] for k in range(8)], 0)
    coupled = halves(dot(jnp.concatenate(rows, axis=0), matrices))
    field = fourths(own_ref[...])

    def add_far(j, table_ref):
        leaf_part = dot(coupled[32 * j : 32 * j + 32], stacked([basis_ref[j]], 0))
        both = dot(field, table_ref[:, 256 * j : 256 * j + 256])
        return leaf_part + both[:32] + both[32:]

    @pl.when(early)
    def _():
        for j in range(4):
            total = begun_ref[j] + add_far(j, early_table_ref)
            for slot, (leaf, t) in enumerate(MISSING):
                if leaf == j:
                    total += dot_nt(window[t], rest_ref[slot])
            near_ref[j] = total

    @pl.when(jnp.logical_not(early))
    def _():
        copies = load_near(cols_hbm, blocks_hbm, cols, blocks, semaphores)
        expand(transfer_ref, basis_ref, late_table_ref)
        near_all(window, cols, blocks, copies, near_ref, first)
        for j in range(4):
            near_ref[j] += add_far(j, late_table_ref)


def product_kernel(
    near_ref, first_ref, odd_ref, even_ref, node_ref, early_table_ref, late_table_ref, out_hbm,
    out, semaphores,
):
    _, early, _ = position()
    is_odd = lax.axis_index("leaf") % 2 == 1
    even = [first_ref[i] + even_ref[i] for i in range(3)]
    given = even[0].astype(F32) + odd_ref[0].astype(F32)
    row = [jnp.where(is_odd, even[i], odd_ref[i]) for i in (1, 2)]
    row += [jnp.where(is_odd, odd_ref[i], even[i]) for i in (1, 2)]
    beside = dot(jnp.concatenate(row, axis=1), stacked([node_ref[0, k] for k in range(4)], 0))
    field = fourths(given[:, :64] + given[:, 64:] + beside)

    def finish(table_ref):
        copies = []
        for j in range(4):
            both = dot(field, table_ref[:, 256 * j : 256 * j + 256])
            out[j] = near_ref[j] + both[:32] + both[32:]
            copies.append(pltpu.make_async_copy(out.at[j], out_hbm.at[j], semaphores.at[j]))
            copies[-1].start()
        for copy in copies:
            copy.wait()

    @pl.when(early)
    def _():
        finish(early_table_ref)

    @pl.when(jnp.logical_not(early))
    def _():
        finish(late_table_ref)


def call(kernel, out, specs, scratch=(), flops=0, size=0, out_spec=VMEM, aliases=()):
    return pl.pallas_call(
        kernel,
        out_shape=[jax.ShapeDtypeStruct(shape, dtype) for shape, dtype in out],
        in_specs=specs,
        out_specs=out_spec if isinstance(out_spec, list) else [out_spec] * len(out),
        input_output_aliases=dict(aliases),
        scratch_shapes=list(scratch),
        compiler_params=pltpu.CompilerParams(vmem_limit_bytes=16 << 20),
        cost_estimate=pl.CostEstimate(flops=flops, bytes_accessed=size, transcendentals=0),
    )


def in_hbm(*arrays):
    return [pltpu.with_memory_space_constraint(array, pltpu.HBM) for array in arrays]


def permute(value, partner, taking=lambda i: True):
    members = lax.axis_size(AXES)
    pairs = [(i, partner(i) % members) for i in range(members) if taking(i)]
    return lax.ppermute(value, AXES, pairs)


def local(
    input_point_values,
    leaf_cluster_basis,
    near_blocks,
    near_cols,
    leaf_transfer,
    leaf_coupling,
    node_coupling,
    level_transfer,
    level_coupling,
):
    block = lax.axis_size("near")
    x, basis, transfer, chunk, package, other_package, level, coupling, leaf, node = call(
        moments_kernel,
        [
            ((4, 32, 256), BF16),
            ((4, 64, 256), BF16),
            ((4, 64, 64), BF16),
            ((block, 32, 128), BF16),
            ((5, 32, 256), BF16),
            ((5, 32, 256), BF16),
            ((3, 2, 64, 64), BF16),
            ((768, 128), BF16),
            ((8, 64, 64), BF16),
            ((1, 4, 64, 64), BF16),
        ],
        [HBM] * 7,
        [
            pltpu.VMEM((3, 4, 64, 64), BF16),
            pltpu.VMEM((block, 32, 128), BF16),
            pltpu.SemaphoreType.DMA((8,)),
        ],
        out_spec=[VMEM] * 3 + [HBM] + [VMEM] * 6,
    )(
        *in_hbm(
            input_point_values,
            leaf_cluster_basis,
            leaf_transfer,
            level_transfer,
            level_coupling,
            leaf_coupling,
            node_coupling,
        )
    )
    begun, rest, early_table = call(
        early_kernel,
        [((4, 32, 256), F32), ((12, 256, 256), BF16), ((128, 1024), BF16)],
        [VMEM] * 3 + [HBM] * 2,
        [
            pltpu.VMEM((10, 32, 256), BF16),
            pltpu.SMEM((4, 7), jnp.int32),
            pltpu.VMEM((4, 7, 256, 256), BF16),
            pltpu.SemaphoreType.DMA((5,)),
        ],
    )(x, transfer, basis, *in_hbm(near_cols, near_blocks))
    chunk, begun, package, other_package = lax.optimization_barrier(
        (chunk, begun, package, other_package)
    )
    nodes = lax.all_to_all(chunk, "near", 0, 0)
    after = permute(other_package, lambda i: i + 1 if i % 2 else i - 1)
    sibling = permute(package, lambda i: i ^ 1)
    first, odd, even, own = call(
        levels_kernel,
        [((3, 32, 128), BF16), ((3, 32, 128), BF16), ((3, 32, 128), BF16), ((32, 64), F32)],
        [VMEM] * 4,
        [
            pltpu.VMEM((8, 32, 128), BF16),
            pltpu.VMEM((4, 32, 128), BF16),
            pltpu.VMEM((2, 32, 128), BF16),
        ],
    )(nodes, level, coupling, node)

    def to_first(i):
        return i // block == 1 and i % block > 0 or i == 0

    first = permute(first, lambda i: i - block if i // block % 2 else i + block, to_first)
    odd = permute(odd, lambda i: i + block if i // block % 2 else i - block)
    even = permute(
        even, lambda i: i - block if i // block % 2 else i + block, lambda i: not to_first(i)
    )
    near, late_table = call(
        near_kernel,
        [((4, 32, 256), F32), ((128, 1024), BF16)],
        [VMEM] * 10 + [HBM] * 2,
        [
            pltpu.VMEM((10, 32, 256), BF16),
            pltpu.SMEM((4, 7), jnp.int32),
            pltpu.VMEM((4, 7, 256, 256), BF16),
            pltpu.SemaphoreType.DMA((5,)),
        ],
        flops=200_000_000,
        size=4_000_000,
    )(
        x,
        sibling,
        after,
        own,
        leaf,
        transfer,
        basis,
        begun,
        rest,
        early_table,
        *in_hbm(near_cols, near_blocks),
    )
    (out,) = call(
        product_kernel,
        [((4, 32, 256), F32)],
        [VMEM] * 7,
        [pltpu.VMEM((4, 32, 256), F32), pltpu.SemaphoreType.DMA((4,))],
        out_spec=HBM,
    )(near, first, odd, even, node, early_table, late_table)
    return out


def solution(mesh):
    spread = P(AXES)
    placed = (spread, spread, spread, spread, spread, P(), spread, P(), P())
    return jax.shard_map(
        local, mesh=mesh, in_specs=placed, out_specs=spread, check_vma=False
    )
```
